32 devices in a mesh: cam: 8 (over z, y), proj: 4 (over x, core).
Axes of the slice: x: 2, y: 2, z: 4, core: 2. Of those that a mesh axis runs over, the one named last changes fastest.
Arguments:
- transport: bfloat16 [4096, 16384], P('cam', 'proj'), may hold values from -0.125 to 0.125
- test_panel: bfloat16 [16384, 32], P(('proj', 'cam')), may hold values from -6 to 6
Outputs:
- basis: float32 [4096, 32], P('cam')
- coimage: float32 [16384, 32], P(('proj', 'cam'))
The draws below stay inside these ranges and needn't reach their ends.
All inputs are finite; a program needn't handle non-finite values.
Results may differ from the reference program's by a relative error of at most 0.0027.
Values may be sent and summed in bfloat16 or wider, within the bound.
A program may use at most 64 MiB of HBM per device.

```python
import jax
import jax.numpy as jnp
from jax import lax

SLAB = 16384
RANK = 32
ITERS = 2
ROWS = 4096


def spiked(values, rng, source, target, shards_of, factor):
    owner, partner = [(jnp.arange(values.shape[axis_at]) // (values.shape[axis_at] // shards_of)).reshape([-1 if axis == axis_at else 1 for axis in range(values.ndim)]) for axis_at in (source, target)]
    chosen = jax.random.permutation(rng, shards_of)[partner]
    strong = (owner == chosen) | (owner == (partner + shards_of // 2) % shards_of)
    return jnp.where(strong, factor * values, values)


def steps_of(rng, shape, shards, low, high):
    factor_of = 1.0
    for dim, shards_of in shards:
        draws = jax.random.uniform(jax.random.fold_in(jax.random.fold_in(rng, 6), dim), (shards_of,), jnp.float32, low / len(shards), high / len(shards))
        factor_of = factor_of * jnp.repeat(jnp.exp(draws), shape[dim] // shards_of).reshape((-1,) + (1,) * (len(shape) - 1 - dim))
    return factor_of


def bell_draw(stream_key, extent, width, limit, cuts=(), dtype=jnp.bfloat16):
    result = jax.random.normal(stream_key, extent, jnp.float32) * width
    if len(cuts) > 0:
        result = steps_of(stream_key, extent, cuts, -0.22, 0.18) * result
    return jnp.clip(result, min=-limit, max=limit).astype(dtype)


def gaussian_with(stream_key, shape, spread, limit, cuts, heavy, held_as=jnp.bfloat16):
    entries = spread * jax.random.normal(stream_key, shape, jnp.float32)
    if cuts:
        entries = entries * steps_of(stream_key, shape, cuts, -0.22, 0.18)
    return jnp.clip(spiked(entries, jax.random.fold_in(stream_key, 3), *heavy), -limit, limit).astype(held_as)


def setup_inputs(seed: int = 0) -> dict:
    seeds = jax.random.split(jax.random.key(seed), 3)
    return {
        "transport": gaussian_with(seeds[0], (ROWS, SLAB), ROWS ** -0.5, 0.125, ((0, 8), (1, 4)), (0, 1, 8, 2.0)),
        "test_panel": bell_draw(seeds[1], (SLAB, RANK), 1.0, 6.0, ((0, 32),)),
    }


def orthonormal(block, count):
    gram = jnp.dot(block.T.astype(jnp.float32), block.astype(jnp.float32), precision=lax.Precision.HIGHEST, preferred_element_type=jnp.float32) / count
    lower = jnp.linalg.cholesky(gram)
    return jax.scipy.linalg.solve_triangular(lower, block.T, lower=True).T

def reference(transport, test_panel):
    panel = test_panel
    basis = None
    coimage = None
    for step in range(ITERS):
        sketch = jnp.dot(transport.astype(jnp.float32), panel.astype(jnp.float32), preferred_element_type=jnp.float32)
        basis = orthonormal(sketch, ROWS)
        basis_low = basis.astype(jnp.bfloat16)
        coimage = jnp.dot(transport.T.astype(jnp.float32), basis_low.astype(jnp.float32), preferred_element_type=jnp.float32)
        if step + 1 < ITERS:
            panel = coimage.astype(jnp.bfloat16)
    return (basis, coimage)
```

```python
import functools

import jax
import jax.numpy as jnp
from jax import lax
from jax.experimental import pallas as pl
from jax.experimental.pallas import tpu as pltpu
from jax.sharding import PartitionSpec as P

ITERS = 2
MESH = pl.DeviceIdType.MESH
HIGHEST = lax.Precision.HIGHEST
NT = (((1,), (1,)), ((), ()))


def small_gram(block):
    return jnp.dot(block.T, block, precision=HIGHEST, preferred_element_type=jnp.float32)


def apply_factor(gram, block):
    lower = jnp.linalg.cholesky(gram)
    return jax.scipy.linalg.solve_triangular(lower, block.T, lower=True).T


def with_collectives(transport, test_panel):
    total_rows = transport.shape[0] * lax.axis_size("cam")
    panel_piece = test_panel
    for step in range(ITERS):
        partial_sketch = jnp.dot(
            transport,
            lax.all_gather(panel_piece, "cam", axis=0, tiled=True),
            preferred_element_type=jnp.float32,
        )
        sketch = lax.psum(partial_sketch, "proj")
        gram = lax.psum(small_gram(sketch), "cam") / total_rows
        basis = apply_factor(gram, sketch)
        coimage = lax.psum_scatter(
            lax.dot_general(
                transport,
                basis.astype(jnp.bfloat16),
                (((0,), (0,)), ((), ())),
                preferred_element_type=jnp.float32,
            ),
            "cam",
            scatter_dimension=0,
            tiled=True,
        )
        panel_piece = coimage.astype(jnp.bfloat16)
    return basis, coimage


def inverse_factor(gram):
    size = gram.shape[0]
    row = lax.broadcasted_iota(jnp.int32, (size, size), 0)
    col = lax.broadcasted_iota(jnp.int32, (size, size), 1)
    left = gram
    right = jnp.where(row == col, 1.0, 0.0).astype(jnp.float32)
    for k in range(size):
        ratio = left[:, k : k + 1] / left[k : k + 1, k : k + 1]
        ratio = jnp.where(row[:, :1] > k, ratio, 0.0)
        right = right - ratio * right[k : k + 1, :]
        if k + 1 < size:
            left = left - ratio * left[k : k + 1, :]
    pivots = jnp.sum(jnp.where(row == col, left, 0.0), axis=1, keepdims=True)
    return right / jnp.sqrt(pivots)


def kernel(
    cams,
    projs,
    transport_ref,
    panel_ref,
    basis_ref,
    coimage_ref,
    transport,
    panels,
    partials,
    grams,
    outgoing,
    incoming,
    load_sem,
    panel_send,
    panel_recv,
    partial_send,
    partial_recv,
    gram_send,
    gram_recv,
    out_send,
    out_recv,
):
    cam, proj = lax.axis_index("cam"), lax.axis_index("proj")
    rank, piece = panel_ref.shape
    rows = transport.shape[1]

    offsets = sorted(range(1, cams), key=lambda o: -min(o, cams - o))
    cam_peers = [lax.rem(cam + o, cams) for o in offsets]
    proj_peers = [lax.rem(proj + o, projs) for o in range(1, projs)]

    loads = []
    for c in range(cams):
        load = pltpu.make_async_copy(
            transport_ref.at[:, pl.ds(c * piece, piece)], transport.at[c], load_sem.at[c]
        )
        load.start()
        loads.append(load)

    barrier = pltpu.get_barrier_semaphore()
    for peer in cam_peers:
        pl.semaphore_signal(barrier, inc=1, device_id=(peer, proj), device_id_type=MESH)
    for peer in proj_peers:
        pl.semaphore_signal(barrier, inc=1, device_id=(cam, peer), device_id_type=MESH)
    panels[0, cam] = panel_ref[...]
    pl.semaphore_wait(barrier, cams - 1 + projs - 1)

    def send(src, dst, send_sem, recv_sem, device):
        copy = pltpu.make_async_remote_copy(
            src_ref=src,
            dst_ref=dst,
            send_sem=send_sem,
            recv_sem=recv_sem,
            device_id=device,
            device_id_type=MESH,
        )
        copy.start()
        return copy

    def arrived(slot, send_sem, recv_sem, device):
        pltpu.make_async_remote_copy(
            src_ref=slot,
            dst_ref=slot,
            send_sem=send_sem,
            recv_sem=recv_sem,
            device_id=device,
            device_id_type=MESH,
        ).wait_recv()

    sends = []
    for step in range(ITERS):
        for peer in cam_peers:
            slot = panels.at[step, cam]
            sends.append(
                send(slot, slot, panel_send.at[step, peer], panel_recv.at[step, cam], (peer, proj))
            )
        if step == 0:
            for load in loads:
                load.wait()
        total = lax.dot_general(
            transport[cam], panels[step, cam], NT, preferred_element_type=jnp.float32
        )
        for peer in reversed(cam_peers):
            arrived(
                panels.at[step, peer], panel_send.at[step, peer], panel_recv.at[step, peer], (peer, proj)
            )
            total += lax.dot_general(
                transport[peer], panels[step, peer], NT, preferred_element_type=jnp.float32
            )
        row = lax.broadcasted_iota(jnp.int32, (rank, rank), 0)
        col = lax.broadcasted_iota(jnp.int32, (rank, rank), 1)
        eye = jnp.where(row == col, 1.0, 0.0).astype(jnp.float32)
        partials[step, proj] = lax.dot_general(
            eye, total, NT, precision=HIGHEST, preferred_element_type=jnp.float32
        )
        for peer in proj_peers:
            slot = partials.at[step, proj]
            sends.append(
                send(slot, slot, partial_send.at[step, peer], partial_recv.at[step, proj], (cam, peer))
            )
        for peer in proj_peers:
            arrived(
                partials.at[step, peer],
                partial_send.at[step, peer],
                partial_recv.at[step, peer],
                (cam, peer),
            )
        sketch = partials[step, 0]
        for j in range(1, projs):
            sketch += partials[step, j]

        grams[step, cam] = lax.dot_general(
            sketch, sketch, NT, precision=HIGHEST, preferred_element_type=jnp.float32
        )
        for peer in cam_peers:
            slot = grams.at[step, cam]
            sends.append(
                send(slot, slot, gram_send.at[step, peer], gram_recv.at[step, cam], (peer, proj))
            )

        high = sketch.astype(jnp.bfloat16)
        low = (sketch - high.astype(jnp.float32)).astype(jnp.bfloat16)
        both = jnp.concatenate([high, low], axis=0)

        def product(c):
            halves = jnp.dot(both, transport[c], preferred_element_type=jnp.float32)
            return halves[:rank] + halves[rank:]

        for peer in cam_peers:
            outgoing[step, peer] = product(peer)
            sends.append(
                send(
                    outgoing.at[step, peer],
                    incoming.at[step, cam],
                    out_send.at[step, peer],
                    out_recv.at[step, cam],
                    (peer, proj),
                )
            )
        summed = product(cam)

        for peer in cam_peers:
            arrived(grams.at[step, peer], gram_send.at[step, peer], gram_recv.at[step, peer], (peer, proj))
        gram = grams[step, 0]
        for c in range(1, cams):
            gram += grams[step, c]
        inverse = inverse_factor(gram / (rows * cams))
        last = step + 1 == ITERS
        if last:
            basis_ref[...] = jnp.dot(
                inverse, sketch, precision=HIGHEST, preferred_element_type=jnp.float32
            )

        for peer in reversed(cam_peers):
            arrived(incoming.at[step, peer], out_send.at[step, peer], out_recv.at[step, peer], (peer, proj))
            summed += incoming[step, peer]
        coimage = jnp.dot(inverse, summed, precision=HIGHEST, preferred_element_type=jnp.float32)
        if last:
            coimage_ref[...] = coimage
        else:
            panels[step + 1, cam] = coimage.astype(jnp.bfloat16)

    for copy in sends:
        copy.wait_send()


def with_kernel(cams, projs, transport, test_panel):
    rows, columns = transport.shape
    piece, rank = test_panel.shape
    dma = pltpu.SemaphoreType.DMA
    basis, coimage = pl.pallas_call(
        functools.partial(kernel, cams, projs),
        out_shape=(
            jax.ShapeDtypeStruct((rank, rows), jnp.float32),
            jax.ShapeDtypeStruct((rank, piece), jnp.float32),
        ),
        in_specs=[
            pl.BlockSpec(memory_space=pl.ANY),
            pl.BlockSpec(memory_space=pltpu.VMEM),
        ],
        out_specs=(
            pl.BlockSpec(memory_space=pltpu.VMEM),
            pl.BlockSpec(memory_space=pltpu.VMEM),
        ),
        scratch_shapes=[
            pltpu.VMEM((cams, rows, piece), jnp.bfloat16),
            pltpu.VMEM((ITERS, cams, rank, piece), jnp.bfloat16),
            pltpu.VMEM((ITERS, projs, rank, rows), jnp.float32),
            pltpu.VMEM((ITERS, cams, rank, rank), jnp.float32),
            pltpu.VMEM((ITERS, cams, rank, piece), jnp.float32),
            pltpu.VMEM((ITERS, cams, rank, piece), jnp.float32),
            dma((cams,)),
            dma((ITERS, cams)),
            dma((ITERS, cams)),
            dma((ITERS, projs)),
            dma((ITERS, projs)),
            dma((ITERS, cams)),
            dma((ITERS, cams)),
            dma((ITERS, cams)),
            dma((ITERS, cams)),
        ],
        compiler_params=pltpu.CompilerParams(
            collective_id=0, has_side_effects=True, vmem_limit_bytes=60 * 2**20
        ),
        cost_estimate=pl.CostEstimate(
            flops=4 * ITERS * rows * columns * rank,
            bytes_accessed=2 * rows * columns,
            transcendentals=0,
        ),
    )(transport, test_panel.T)
    return basis.T, coimage.T


def solution(mesh):
    cams, projs = mesh.shape["cam"], mesh.shape["proj"]

    def on_device(transport, test_panel):
        if test_panel.shape[0] % 128 or transport.shape[0] % 128:
            return with_collectives(transport, test_panel)
        return with_kernel(cams, projs, transport, test_panel)

    return jax.shard_map(
        on_device,
        mesh=mesh,
        in_specs=(P("cam", "proj"), P(("proj", "cam"), None)),
        out_specs=(P("cam", None), P(("proj", "cam"), None)),
        check_vma=False,
    )
```

```python
import functools

import jax
import jax.numpy as jnp
from jax import lax
from jax.experimental import pallas as pl
from jax.experimental.pallas import tpu as pltpu
from jax.sharding import PartitionSpec as P

ITERS = 2
MESH = pl.DeviceIdType.MESH
HIGHEST = lax.Precision.HIGHEST
NT = (((1,), (1,)), ((), ()))


def small_gram(block):
    return jnp.dot(block.T, block, precision=HIGHEST, preferred_element_type=jnp.float32)


def apply_factor(gram, block):
    lower = jnp.linalg.cholesky(gram)
    return jax.scipy.linalg.solve_triangular(lower, block.T, lower=True).T


def with_collectives(transport, test_panel):
    total_rows = transport.shape[0] * lax.axis_size("cam")
    panel_piece = test_panel
    for step in range(ITERS):
        partial_sketch = jnp.dot(
            transport,
            lax.all_gather(panel_piece, "cam", axis=0, tiled=True),
            preferred_element_type=jnp.float32,
        )
        sketch = lax.psum(partial_sketch, "proj")
        gram = lax.psum(small_gram(sketch), "cam") / total_rows
        basis = apply_factor(gram, sketch)
        coimage = lax.psum_scatter(
            lax.dot_general(
                transport,
                basis.astype(jnp.bfloat16),
                (((0,), (0,)), ((), ())),
                preferred_element_type=jnp.float32,
            ),
            "cam",
            scatter_dimension=0,
            tiled=True,
        )
        panel_piece = coimage.astype(jnp.bfloat16)
    return basis, coimage


def inverse_factor(gram):
    size = gram.shape[0]
    row = lax.broadcasted_iota(jnp.int32, (size, size), 0)
    col = lax.broadcasted_iota(jnp.int32, (size, size), 1)
    left = gram
    right = jnp.where(row == col, 1.0, 0.0).astype(jnp.float32)
    for k in range(size):
        ratio = left[:, k : k + 1] / left[k : k + 1, k : k + 1]
        ratio = jnp.where(row[:, :1] > k, ratio, 0.0)
        right = right - ratio * right[k : k + 1, :]
        if k + 1 < size:
            left = left - ratio * left[k : k + 1, :]
    pivots = jnp.sum(jnp.where(row == col, left, 0.0), axis=1, keepdims=True)
    return right / jnp.sqrt(pivots)


def kernel(
    cams,
    projs,
    transport_ref,
    panel_ref,
    basis_ref,
    coimage_ref,
    transport,
    panels,
    partials,
    grams,
    pair_out,
    pair_in,
    line_out,
    line_in,
    load_sem,
    panel_send,
    panel_recv,
    partial_send,
    partial_recv,
    gram_send,
    gram_recv,
    pair_send,
    pair_recv,
    line_send,
    line_recv,
):
    cam, proj = lax.axis_index("cam"), lax.axis_index("proj")
    rank, piece = panel_ref.shape
    rows = transport.shape[1]

    spots = cams // 2
    spot, side = cam // 2, lax.rem(cam, 2)
    other = 1 - side
    pair = 2 * spot + other
    offsets = sorted(range(1, spots), key=lambda o: -min(o, spots - o))
    line = [lax.rem(spot + o, spots) for o in offsets]
    cam_peers = [lax.rem(cam + o, cams) for o in range(1, cams)]
    proj_peers = [lax.rem(proj + o, projs) for o in range(1, projs)]

    loads = []
    for c in range(cams):
        load = pltpu.make_async_copy(
            transport_ref.at[:, pl.ds(c * piece, piece)], transport.at[c], load_sem.at[c]
        )
        load.start()
        loads.append(load)

    barrier = pltpu.get_barrier_semaphore()
    for peer in cam_peers:
        pl.semaphore_signal(barrier, inc=1, device_id=(peer, proj), device_id_type=MESH)
    for peer in proj_peers:
        pl.semaphore_signal(barrier, inc=1, device_id=(cam, peer), device_id_type=MESH)
    panels[0, cam] = panel_ref[...]
    pl.semaphore_wait(barrier, cams - 1 + projs - 1)

    sends = []

    def send(src, dst, send_sem, recv_sem, device):
        copy = pltpu.make_async_remote_copy(
            src_ref=src,
            dst_ref=dst,
            send_sem=send_sem,
            recv_sem=recv_sem,
            device_id=device,
            device_id_type=MESH,
        )
        copy.start()
        sends.append(copy)

    def arrived(slot, send_sem, recv_sem):
        pltpu.make_async_remote_copy(
            src_ref=slot,
            dst_ref=slot,
            send_sem=send_sem,
            recv_sem=recv_sem,
            device_id=(pair, proj),
            device_id_type=MESH,
        ).wait_recv()

    for step in range(ITERS):

        def share(c, peer, sem):
            slot = panels.at[step, c]
            send(slot, slot, panel_send.at[step, sem], panel_recv.at[step, c], (peer, proj))

        def sketched(c):
            return lax.dot_general(
                transport[c], panels[step, c], NT, preferred_element_type=jnp.float32
            )

        def wait_panel(c):
            arrived(panels.at[step, c], panel_send.at[step, c], panel_recv.at[step, c])

        for s in line:
            share(cam, 2 * s + side, 2 * s + side)
        share(cam, pair, pair)
        if step == 0:
            for load in loads:
                load.wait()
        total = sketched(cam)
        for s in reversed(line):
            wait_panel(2 * s + side)
            share(2 * s + side, pair, 2 * s + other)
            total += sketched(2 * s + side)
        wait_panel(pair)
        total += sketched(pair)
        for s in reversed(line):
            wait_panel(2 * s + other)
            total += sketched(2 * s + other)

        row = lax.broadcasted_iota(jnp.int32, (rank, rank), 0)
        col = lax.broadcasted_iota(jnp.int32, (rank, rank), 1)
        eye = jnp.where(row == col, 1.0, 0.0).astype(jnp.float32)
        partials[step, proj] = lax.dot_general(
            eye, total, NT, precision=HIGHEST, preferred_element_type=jnp.float32
        )
        for peer in proj_peers:
            slot = partials.at[step, proj]
            send(slot, slot, partial_send.at[step, peer], partial_recv.at[step, proj], (cam, peer))
        for peer in proj_peers:
            arrived(partials.at[step, peer], partial_send.at[step, peer], partial_recv.at[step, peer])
        sketch = partials[step, 0]
        for j in range(1, projs):
            sketch += partials[step, j]

        high = sketch.astype(jnp.bfloat16)
        low = (sketch - high.astype(jnp.float32)).astype(jnp.bfloat16)
        both = jnp.concatenate([high, low], axis=0)

        def product(c):
            halves = jnp.dot(both, transport[c], preferred_element_type=jnp.float32)
            return halves[:rank] + halves[rank:]

        def to_pair(s):
            pair_out[step, s] = product(2 * s + other)
            send(
                pair_out.at[step, s],
                pair_in.at[step, s],
                pair_send.at[step, s],
                pair_recv.at[step, s],
                (pair, proj),
            )

        def from_pair(s):
            arrived(pair_in.at[step, s], pair_send.at[step, s], pair_recv.at[step, s])
            return pair_in[step, s]

        to_pair(line[0])
        gram = lax.dot_general(
            sketch, sketch, NT, precision=HIGHEST, preferred_element_type=jnp.float32
        )
        folds = 128 // rank
        tall = rank // folds
        grams[step, cam] = jnp.concatenate(
            [gram[f * tall : (f + 1) * tall] for f in range(folds)], axis=1
        )
        for peer in cam_peers:
            slot = grams.at[step, cam]
            send(slot, slot, gram_send.at[step, peer], gram_recv.at[step, cam], (peer, proj))
        for s in line[1:] + [spot]:
            to_pair(s)
        for s in line:
            mine = product(2 * s + side)
            line_out[step, s] = mine + from_pair(s)
            send(
                line_out.at[step, s],
                line_in.at[step, spot],
                line_send.at[step, s],
                line_recv.at[step, spot],
                (2 * s + side, proj),
            )
        summed = product(cam) + from_pair(spot)

        for peer in cam_peers:
            arrived(grams.at[step, peer], gram_send.at[step, peer], gram_recv.at[step, peer])
        folded = grams[step, 0]
        for c in range(1, cams):
            folded += grams[step, c]
        folded = folded / (rows * cams)
        inverse = inverse_factor(
            jnp.concatenate([folded[:, f * rank : (f + 1) * rank] for f in range(folds)], axis=0)
        )
        last = step + 1 == ITERS
        if last:
            basis_ref[...] = jnp.dot(
                inverse, sketch, precision=HIGHEST, preferred_element_type=jnp.float32
            )

        for s in reversed(line):
            arrived(line_in.at[step, s], line_send.at[step, s], line_recv.at[step, s])
            summed += line_in[step, s]
        coimage = jnp.dot(inverse, summed, precision=HIGHEST, preferred_element_type=jnp.float32)
        if last:
            coimage_ref[...] = coimage
        else:
            panels[step + 1, cam] = coimage.astype(jnp.bfloat16)

    for copy in sends:
        copy.wait_send()


def deliver(basis_ref, coimage_ref, basis_out, coimage_out, sem):
    first = pltpu.make_async_copy(basis_ref, basis_out, sem.at[0])
    second = pltpu.make_async_copy(coimage_ref, coimage_out, sem.at[1])
    first.start()
    second.start()
    first.wait()
    second.wait()


def with_kernel(cams, projs, transport, test_panel):
    rows, columns = transport.shape
    piece, rank = test_panel.shape
    dma = pltpu.SemaphoreType.DMA
    in_vmem = pl.BlockSpec(memory_space=pltpu.VMEM)
    anywhere = pl.BlockSpec(memory_space=pl.ANY)
    results = (
        jax.ShapeDtypeStruct((rank, rows), jnp.float32),
        jax.ShapeDtypeStruct((rank, piece), jnp.float32),
    )
    exchanged = pltpu.VMEM((ITERS, cams // 2, rank, piece), jnp.float32)
    basis, coimage = pl.pallas_call(
        functools.partial(kernel, cams, projs),
        out_shape=results,
        in_specs=[anywhere, in_vmem],
        out_specs=(in_vmem, in_vmem),
        scratch_shapes=[
            pltpu.VMEM((cams, rows, piece), jnp.bfloat16),
            pltpu.VMEM((ITERS, cams, rank, piece), jnp.bfloat16),
            pltpu.VMEM((ITERS, projs, rank, rows), jnp.float32),
            pltpu.VMEM((ITERS, cams, rank * rank // 128, 128), jnp.float32),
            exchanged,
            exchanged,
            exchanged,
            exchanged,
            dma((cams,)),
            dma((ITERS, cams)),
            dma((ITERS, cams)),
            dma((ITERS, projs)),
            dma((ITERS, projs)),
            dma((ITERS, cams)),
            dma((ITERS, cams)),
            dma((ITERS, cams // 2)),
            dma((ITERS, cams // 2)),
            dma((ITERS, cams // 2)),
            dma((ITERS, cams // 2)),
        ],
        compiler_params=pltpu.CompilerParams(
            collective_id=0, has_side_effects=True, vmem_limit_bytes=60 * 2**20
        ),
        cost_estimate=pl.CostEstimate(
            flops=4 * ITERS * rows * columns * rank,
            bytes_accessed=2 * rows * columns,
            transcendentals=0,
        ),
    )(transport, test_panel.T)
    basis, coimage = pl.pallas_call(
        deliver,
        out_shape=results,
        in_specs=[anywhere, anywhere],
        out_specs=(anywhere, anywhere),
        scratch_shapes=[dma((2,))],
    )(basis, coimage)
    return basis.T, coimage.T


def solution(mesh):
    cams, projs = mesh.shape["cam"], mesh.shape["proj"]

    def on_device(transport, test_panel):
        if test_panel.shape[0] % 128 or transport.shape[0] % 128 or cams % 2:
            return with_collectives(transport, test_panel)
        return with_kernel(cams, projs, transport, test_panel)

    return jax.shard_map(
        on_device,
        mesh=mesh,
        in_specs=(P("cam", "proj"), P(("proj", "cam"), None)),
        out_specs=(P("cam", None), P(("proj", "cam"), None)),
        check_vma=False,
    )
```

```python
import functools

import jax
import jax.numpy as jnp
from jax import lax
from jax.experimental import pallas as pl
from jax.experimental.pallas import tpu as pltpu
from jax.sharding import PartitionSpec as P

ITERS = 2
HALVES = 2
MESH = pl.DeviceIdType.MESH
HIGHEST = lax.Precision.HIGHEST
NT = (((1,), (1,)), ((), ()))


def small_gram(block):
    return jnp.dot(block.T, block, precision=HIGHEST, preferred_element_type=jnp.float32)


def apply_factor(gram, block):
    lower = jnp.linalg.cholesky(gram)
    return jax.scipy.linalg.solve_triangular(lower, block.T, lower=True).T


def with_collectives(transport, test_panel):
    total_rows = transport.shape[0] * lax.axis_size("cam")
    panel_piece = test_panel
    for step in range(ITERS):
        partial_sketch = jnp.dot(
            transport,
            lax.all_gather(panel_piece, "cam", axis=0, tiled=True),
            preferred_element_type=jnp.float32,
        )
        sketch = lax.psum(partial_sketch, "proj")
        gram = lax.psum(small_gram(sketch), "cam") / total_rows
        basis = apply_factor(gram, sketch)
        coimage = lax.psum_scatter(
            lax.dot_general(
                transport,
                basis.astype(jnp.bfloat16),
                (((0,), (0,)), ((), ())),
                preferred_element_type=jnp.float32,
            ),
            "cam",
            scatter_dimension=0,
            tiled=True,
        )
        panel_piece = coimage.astype(jnp.bfloat16)
    return basis, coimage


def inverse_factor(gram):
    size = gram.shape[0]
    row = lax.broadcasted_iota(jnp.int32, (size, size), 0)
    col = lax.broadcasted_iota(jnp.int32, (size, size), 1)
    left = gram
    right = jnp.where(row == col, 1.0, 0.0).astype(jnp.float32)
    for k in range(size):
        ratio = left[:, k : k + 1] / left[k : k + 1, k : k + 1]
        ratio = jnp.where(row[:, :1] > k, ratio, 0.0)
        right = right - ratio * right[k : k + 1, :]
        if k + 1 < size:
            left = left - ratio * left[k : k + 1, :]
    pivots = jnp.sum(jnp.where(row == col, left, 0.0), axis=1, keepdims=True)
    return right / jnp.sqrt(pivots)


def kernel(
    cams,
    projs,
    transport_ref,
    panel_ref,
    basis_ref,
    coimage_ref,
    transport,
    panels,
    partials,
    grams,
    pair_out,
    pair_in,
    line_out,
    line_in,
    load_sem,
    panel_send,
    panel_recv,
    partial_send,
    partial_recv,
    gram_send,
    gram_recv,
    pair_send,
    pair_recv,
    line_send,
    line_recv,
):
    cam, proj = lax.axis_index("cam"), lax.axis_index("proj")
    rank, piece = panel_ref.shape
    rows = transport.shape[1]

    spots = cams // 2
    spot, side = cam // 2, lax.rem(cam, 2)
    other = 1 - side
    pair = 2 * spot + other
    offsets = sorted(range(1, spots), key=lambda o: -min(o, spots - o))
    line = [lax.rem(spot + o, spots) for o in offsets]
    cam_peers = [lax.rem(cam + o, cams) for o in range(1, cams)]
    proj_peers = [lax.rem(proj + o, projs) for o in range(1, projs)]

    loads = []
    for c in range(cams):
        load = pltpu.make_async_copy(
            transport_ref.at[:, pl.ds(c * piece, piece)], transport.at[c], load_sem.at[c]
        )
        load.start()
        loads.append(load)

    barrier = pltpu.get_barrier_semaphore()
    for peer in cam_peers:
        pl.semaphore_signal(barrier, inc=1, device_id=(peer, proj), device_id_type=MESH)
    for peer in proj_peers:
        pl.semaphore_signal(barrier, inc=1, device_id=(cam, peer), device_id_type=MESH)
    for i in range(HALVES):
        panels[i, cam] = panel_ref[i * (rank // HALVES) : (i + 1) * (rank // HALVES), :]
    pl.semaphore_wait(barrier, cams - 1 + projs - 1)

    sends = []

    def send(src, dst, send_sem, recv_sem, device):
        copy = pltpu.make_async_remote_copy(
            src_ref=src,
            dst_ref=dst,
            send_sem=send_sem,
            recv_sem=recv_sem,
            device_id=device,
            device_id_type=MESH,
        )
        copy.start()
        sends.append(copy)

    def arrived(slot, send_sem, recv_sem):
        pltpu.make_async_remote_copy(
            src_ref=slot,
            dst_ref=slot,
            send_sem=send_sem,
            recv_sem=recv_sem,
            device_id=(pair, proj),
            device_id_type=MESH,
        ).wait_recv()

    width = rank // HALVES
    row = lax.broadcasted_iota(jnp.int32, (width, width), 0)
    col = lax.broadcasted_iota(jnp.int32, (width, width), 1)
    eye = jnp.where(row == col, 1.0, 0.0).astype(jnp.float32)

    def share(q, c, peer, sem):
        slot = panels.at[q, c]
        send(slot, slot, panel_send.at[q, sem], panel_recv.at[q, c], (peer, proj))

    def wait_panel(q, c):
        arrived(panels.at[q, c], panel_send.at[q, c], panel_recv.at[q, c])

    def sketched(q, c):
        return lax.dot_general(
            transport[c], panels[q, c], NT, preferred_element_type=jnp.float32
        )

    def product(both, c):
        halves = jnp.dot(both, transport[c], preferred_element_type=jnp.float32)
        return halves[:width] + halves[width:]

    def to_pair(q, both, s):
        pair_out[q, s] = product(both, 2 * s + other)
        send(
            pair_out.at[q, s],
            pair_in.at[q, s],
            pair_send.at[q, s],
            pair_recv.at[q, s],
            (pair, proj),
        )

    def from_pair(q, s):
        arrived(pair_in.at[q, s], pair_send.at[q, s], pair_recv.at[q, s])
        return pair_in[q, s]

    def to_line(q, both, s):
        line_out[q, s] = product(both, 2 * s + side) + from_pair(q, s)
        send(
            line_out.at[q, s],
            line_in.at[q, spot],
            line_send.at[q, s],
            line_recv.at[q, spot],
            (2 * s + side, proj),
        )

    for step in range(ITERS):
        parts = range(step * HALVES, (step + 1) * HALVES)
        for q in parts:
            for s in line:
                share(q, cam, 2 * s + side, 2 * s + side)
            share(q, cam, pair, pair)
        if step == 0:
            for load in loads:
                load.wait()
        totals = []
        for q in parts:
            total = sketched(q, cam)
            for s in reversed(line):
                wait_panel(q, 2 * s + side)
                share(q, 2 * s + side, pair, 2 * s + other)
                total += sketched(q, 2 * s + side)
            totals.append(total)
        for q, total in zip(parts, totals):
            wait_panel(q, pair)
            total += sketched(q, pair)
            for s in reversed(line):
                wait_panel(q, 2 * s + other)
                total += sketched(q, 2 * s + other)
            partials[q, proj] = lax.dot_general(
                eye, total, NT, precision=HIGHEST, preferred_element_type=jnp.float32
            )
            for peer in proj_peers:
                slot = partials.at[q, proj]
                send(slot, slot, partial_send.at[q, peer], partial_recv.at[q, proj], (cam, peer))

        sketches = []
        split = []
        for q in parts:
            for peer in proj_peers:
                arrived(partials.at[q, peer], partial_send.at[q, peer], partial_recv.at[q, peer])
            sketch = partials[q, 0]
            for j in range(1, projs):
                sketch += partials[q, j]
            high = sketch.astype(jnp.bfloat16)
            low = (sketch - high.astype(jnp.float32)).astype(jnp.bfloat16)
            sketches.append(sketch)
            split.append(jnp.concatenate([high, low], axis=0))
            for s in line + [spot]:
                to_pair(q, split[-1], s)
                if len(split) > 1 and s is not spot:
                    to_line(q - 1, split[-2], s)
        for s in line:
            to_line(parts[-1], split[-1], s)

        sketch = jnp.concatenate(sketches, axis=0)
        gram = lax.dot_general(
            sketch, sketch, NT, precision=HIGHEST, preferred_element_type=jnp.float32
        )
        folds = 128 // rank
        tall = rank // folds
        grams[step, cam] = jnp.concatenate(
            [gram[f * tall : (f + 1) * tall] for f in range(folds)], axis=1
        )
        for peer in cam_peers:
            slot = grams.at[step, cam]
            send(slot, slot, gram_send.at[step, peer], gram_recv.at[step, cam], (peer, proj))
        sums = [product(both, cam) + from_pair(q, spot) for q, both in zip(parts, split)]

        for peer in cam_peers:
            arrived(grams.at[step, peer], gram_send.at[step, peer], gram_recv.at[step, peer])
        folded = grams[step, 0]
        for c in range(1, cams):
            folded += grams[step, c]
        folded = folded / (rows * cams)
        inverse = inverse_factor(
            jnp.concatenate([folded[:, f * rank : (f + 1) * rank] for f in range(folds)], axis=0)
        )
        last = step + 1 == ITERS
        if last:
            basis_ref[...] = jnp.dot(
                inverse, sketch, precision=HIGHEST, preferred_element_type=jnp.float32
            )

        for i, q in enumerate(parts):
            for s in reversed(line):
                arrived(line_in.at[q, s], line_send.at[q, s], line_recv.at[q, s])
                sums[i] += line_in[q, s]
        coimage = jnp.dot(
            inverse,
            jnp.concatenate(sums, axis=0),
            precision=HIGHEST,
            preferred_element_type=jnp.float32,
        )
        if last:
            coimage_ref[...] = coimage
        else:
            for i in range(HALVES):
                panels[parts[-1] + 1 + i, cam] = coimage[i * width : (i + 1) * width].astype(
                    jnp.bfloat16
                )

    for copy in sends:
        copy.wait_send()


def deliver(basis_ref, coimage_ref, basis_out, coimage_out, basis, coimage, sem):
    reads = [
        pltpu.make_async_copy(basis_ref, basis, sem.at[0]),
        pltpu.make_async_copy(coimage_ref, coimage, sem.at[1]),
    ]
    writes = [
        pltpu.make_async_copy(basis, basis_out, sem.at[2]),
        pltpu.make_async_copy(coimage, coimage_out, sem.at[3]),
    ]
    for read in reads:
        read.start()
    for read, write in zip(reads, writes):
        read.wait()
        write.start()
    for write in writes:
        write.wait()


def with_kernel(cams, projs, transport, test_panel):
    rows, columns = transport.shape
    piece, rank = test_panel.shape
    dma = pltpu.SemaphoreType.DMA
    in_vmem = pl.BlockSpec(memory_space=pltpu.VMEM)
    anywhere = pl.BlockSpec(memory_space=pl.ANY)
    results = (
        jax.ShapeDtypeStruct((rank, rows), jnp.float32),
        jax.ShapeDtypeStruct((rank, piece), jnp.float32),
    )
    width = rank // HALVES
    parts = ITERS * HALVES
    exchanged = pltpu.VMEM((parts, cams // 2, width, piece), jnp.float32)
    basis, coimage = pl.pallas_call(
        functools.partial(kernel, cams, projs),
        out_shape=results,
        in_specs=[anywhere, in_vmem],
        out_specs=(in_vmem, in_vmem),
        scratch_shapes=[
            pltpu.VMEM((cams, rows, piece), jnp.bfloat16),
            pltpu.VMEM((parts, cams, width, piece), jnp.bfloat16),
            pltpu.VMEM((parts, projs, width, rows), jnp.float32),
            pltpu.VMEM((ITERS, cams, rank * rank // 128, 128), jnp.float32),
            exchanged,
            exchanged,
            exchanged,
            exchanged,
            dma((cams,)),
            dma((parts, cams)),
            dma((parts, cams)),
            dma((parts, projs)),
            dma((parts, projs)),
            dma((ITERS, cams)),
            dma((ITERS, cams)),
            dma((parts, cams // 2)),
            dma((parts, cams // 2)),
            dma((parts, cams // 2)),
            dma((parts, cams // 2)),
        ],
        compiler_params=pltpu.CompilerParams(
            collective_id=0, has_side_effects=True, vmem_limit_bytes=60 * 2**20
        ),
        cost_estimate=pl.CostEstimate(
            flops=4 * ITERS * rows * columns * rank,
            bytes_accessed=2 * rows * columns,
            transcendentals=0,
        ),
    )(transport, test_panel.T)
    basis, coimage = pl.pallas_call(
        deliver,
        out_shape=results,
        in_specs=[anywhere, anywhere],
        out_specs=(anywhere, anywhere),
        scratch_shapes=[
            pltpu.VMEM((rank, rows), jnp.float32),
            pltpu.VMEM((rank, piece), jnp.float32),
            dma((4,)),
        ],
    )(basis, coimage)
    return basis.T, coimage.T


def solution(mesh):
    cams, projs = mesh.shape["cam"], mesh.shape["proj"]

    def on_device(transport, test_panel):
        if test_panel.shape[0] % 128 or transport.shape[0] % 128 or cams % 2:
            return with_collectives(transport, test_panel)
        return with_kernel(cams, projs, transport, test_panel)

    return jax.shard_map(
        on_device,
        mesh=mesh,
        in_specs=(P("cam", "proj"), P(("proj", "cam"), None)),
        out_specs=(P("cam", None), P(("proj", "cam"), None)),
        check_vma=False,
    )
```

```python
import functools

import jax
import jax.numpy as jnp
from jax import lax
from jax.experimental import pallas as pl
from jax.experimental.pallas import tpu as pltpu
from jax.sharding import PartitionSpec as P

ITERS = 2
MESH = pl.DeviceIdType.MESH
HIGHEST = lax.Precision.HIGHEST
NT = (((1,), (1,)), ((), ()))


def small_gram(block):
    return jnp.dot(block.T, block, precision=HIGHEST, preferred_element_type=jnp.float32)


def apply_factor(gram, block):
    lower = jnp.linalg.cholesky(gram)
    return jax.scipy.linalg.solve_triangular(lower, block.T, lower=True).T


def with_collectives(transport, test_panel):
    total_rows = transport.shape[0] * lax.axis_size("cam")
    panel_piece = test_panel
    for step in range(ITERS):
        partial_sketch = jnp.dot(
            transport,
            lax.all_gather(panel_piece, "cam", axis=0, tiled=True),
            preferred_element_type=jnp.float32,
        )
        sketch = lax.psum(partial_sketch, "proj")
        gram = lax.psum(small_gram(sketch), "cam") / total_rows
        basis = apply_factor(gram, sketch)
        coimage = lax.psum_scatter(
            lax.dot_general(
                transport,
                basis.astype(jnp.bfloat16),
                (((0,), (0,)), ((), ())),
                preferred_element_type=jnp.float32,
            ),
            "cam",
            scatter_dimension=0,
            tiled=True,
        )
        panel_piece = coimage.astype(jnp.bfloat16)
    return basis, coimage


def inverse_factor(gram):
    size = gram.shape[0]
    row = lax.broadcasted_iota(jnp.int32, (size, size), 0)
    col = lax.broadcasted_iota(jnp.int32, (size, size), 1)
    left = gram
    right = jnp.where(row == col, 1.0, 0.0).astype(jnp.float32)
    for k in range(size):
        ratio = left[:, k : k + 1] / left[k : k + 1, k : k + 1]
        ratio = jnp.where(row[:, :1] > k, ratio, 0.0)
        right = right - ratio * right[k : k + 1, :]
        if k + 1 < size:
            left = left - ratio * left[k : k + 1, :]
    pivots = jnp.sum(jnp.where(row == col, left, 0.0), axis=1, keepdims=True)
    return right / jnp.sqrt(pivots)


def kernel(
    cams,
    projs,
    transport_ref,
    panel_ref,
    basis_ref,
    coimage_ref,
    transport,
    panels,
    partials,
    grams,
    pair_out,
    pair_in,
    line_out,
    line_in,
    load_sem,
    panel_send,
    panel_recv,
    partial_send,
    partial_recv,
    gram_send,
    gram_recv,
    pair_send,
    pair_recv,
    line_send,
    line_recv,
):
    cam, proj = lax.axis_index("cam"), lax.axis_index("proj")
    rank, piece = panel_ref.shape
    rows = transport.shape[1]

    spots = cams // 2
    spot, side = cam // 2, lax.rem(cam, 2)
    other = 1 - side
    pair = 2 * spot + other
    offsets = sorted(range(1, spots), key=lambda o: -min(o, spots - o))
    line = [lax.rem(spot + o, spots) for o in offsets]
    cam_peers = [lax.rem(cam + o, cams) for o in range(1, cams)]
    proj_peers = [lax.rem(proj + o, projs) for o in range(1, projs)]

    loads = []
    for c in range(cams):
        load = pltpu.make_async_copy(
            transport_ref.at[:, pl.ds(c * piece, piece)], transport.at[c], load_sem.at[c]
        )
        load.start()
        loads.append(load)

    barrier = pltpu.get_barrier_semaphore()
    for peer in cam_peers:
        pl.semaphore_signal(barrier, inc=1, device_id=(peer, proj), device_id_type=MESH)
    for peer in proj_peers:
        pl.semaphore_signal(barrier, inc=1, device_id=(cam, peer), device_id_type=MESH)
    panels[0, cam] = panel_ref[...]
    pl.semaphore_wait(barrier, cams - 1 + projs - 1)

    def copy_of(src, dst, send_sem, recv_sem, device):
        return pltpu.make_async_remote_copy(
            src_ref=src,
            dst_ref=dst,
            send_sem=send_sem,
            recv_sem=recv_sem,
            device_id=device,
            device_id_type=MESH,
        )

    def arrived(slot, send_sem, recv_sem):
        copy_of(slot, slot, send_sem, recv_sem, (pair, proj)).wait_recv()

    folds = 128 // rank
    tall = rank // folds

    def one_pass(step, carry):
        sends = []

        def send(*parts):
            copy = copy_of(*parts)
            copy.start()
            sends.append(copy)

        def share(c, peer, sem):
            slot = panels.at[step, c]
            send(slot, slot, panel_send.at[step, sem], panel_recv.at[step, c], (peer, proj))

        def wait_panel(c):
            arrived(panels.at[step, c], panel_send.at[step, c], panel_recv.at[step, c])

        def sketched(c):
            return lax.dot_general(
                panels[step, c], transport[c], NT, preferred_element_type=jnp.float32
            )

        for s in line:
            share(cam, 2 * s + side, 2 * s + side)
        share(cam, pair, pair)

        @pl.when(step == 0)
        def _():
            for load in loads:
                load.wait()

        total = sketched(cam)
        for s in reversed(line):
            wait_panel(2 * s + side)
            share(2 * s + side, pair, 2 * s + other)
            total += sketched(2 * s + side)
        wait_panel(pair)
        total += sketched(pair)
        for s in reversed(line):
            wait_panel(2 * s + other)
            total += sketched(2 * s + other)
        partials[step, proj] = total
        for peer in proj_peers:
            slot = partials.at[step, proj]
            send(slot, slot, partial_send.at[step, peer], partial_recv.at[step, proj], (cam, peer))
        for peer in proj_peers:
            arrived(partials.at[step, peer], partial_send.at[step, peer], partial_recv.at[step, peer])
        sketch = partials[step, 0]
        for j in range(1, projs):
            sketch += partials[step, j]

        high = sketch.astype(jnp.bfloat16)
        low = (sketch - high.astype(jnp.float32)).astype(jnp.bfloat16)
        both = jnp.concatenate([high, low], axis=0)

        def product(c):
            halves = jnp.dot(both, transport[c], preferred_element_type=jnp.float32)
            return halves[:rank] + halves[rank:]

        def to_pair(s):
            pair_out[step, s] = product(2 * s + other)
            send(
                pair_out.at[step, s],
                pair_in.at[step, s],
                pair_send.at[step, s],
                pair_recv.at[step, s],
                (pair, proj),
            )

        def from_pair(s):
            arrived(pair_in.at[step, s], pair_send.at[step, s], pair_recv.at[step, s])
            return pair_in[step, s]

        for s in line:
            to_pair(s)
        gram = lax.dot_general(
            sketch, sketch, NT, precision=HIGHEST, preferred_element_type=jnp.float32
        )
        grams[step, cam] = jnp.concatenate(
            [gram[f * tall : (f + 1) * tall] for f in range(folds)], axis=1
        )
        for peer in cam_peers:
            slot = grams.at[step, cam]
            send(slot, slot, gram_send.at[step, peer], gram_recv.at[step, cam], (peer, proj))
        to_pair(spot)
        for s in line:
            line_out[step, s] = product(2 * s + side) + from_pair(s)
            send(
                line_out.at[step, s],
                line_in.at[step, spot],
                line_send.at[step, s],
                line_recv.at[step, spot],
                (2 * s + side, proj),
            )
        summed = product(cam) + from_pair(spot)

        for peer in cam_peers:
            arrived(grams.at[step, peer], gram_send.at[step, peer], gram_recv.at[step, peer])
        folded = grams[step, 0]
        for c in range(1, cams):
            folded += grams[step, c]
        folded = folded / (rows * cams)
        inverse = inverse_factor(
            jnp.concatenate([folded[:, f * rank : (f + 1) * rank] for f in range(folds)], axis=0)
        )
        basis_ref[...] = jnp.dot(
            inverse, sketch, precision=HIGHEST, preferred_element_type=jnp.float32
        )

        for s in reversed(line):
            arrived(line_in.at[step, s], line_send.at[step, s], line_recv.at[step, s])
            summed += line_in[step, s]
        coimage = jnp.dot(inverse, summed, precision=HIGHEST, preferred_element_type=jnp.float32)
        coimage_ref[...] = coimage
        panels[step + 1, cam] = coimage.astype(jnp.bfloat16)
        for copy in sends:
            copy.wait_send()
        return carry

    lax.fori_loop(0, ITERS, one_pass, 0)


def deliver(basis_ref, coimage_ref, basis_out, coimage_out, basis, coimage, sem):
    reads = [
        pltpu.make_async_copy(basis_ref, basis, sem.at[0]),
        pltpu.make_async_copy(coimage_ref, coimage, sem.at[1]),
    ]
    writes = [
        pltpu.make_async_copy(basis, basis_out, sem.at[2]),
        pltpu.make_async_copy(coimage, coimage_out, sem.at[3]),
    ]
    for read in reads:
        read.start()
    for read, write in zip(reads, writes):
        read.wait()
        write.start()
    for write in writes:
        write.wait()


def with_kernel(cams, projs, transport, test_panel):
    rows, columns = transport.shape
    piece, rank = test_panel.shape
    dma = pltpu.SemaphoreType.DMA
    in_vmem = pl.BlockSpec(memory_space=pltpu.VMEM)
    anywhere = pl.BlockSpec(memory_space=pl.ANY)
    results = (
        jax.ShapeDtypeStruct((rank, rows), jnp.float32),
        jax.ShapeDtypeStruct((rank, piece), jnp.float32),
    )
    exchanged = pltpu.VMEM((ITERS, cams // 2, rank, piece), jnp.float32)
    basis, coimage = pl.pallas_call(
        functools.partial(kernel, cams, projs),
        out_shape=results,
        in_specs=[anywhere, in_vmem],
        out_specs=(in_vmem, in_vmem),
        scratch_shapes=[
            pltpu.VMEM((cams, rows, piece), jnp.bfloat16),
            pltpu.VMEM((ITERS + 1, cams, rank, piece), jnp.bfloat16),
            pltpu.VMEM((ITERS, projs, rank, rows), jnp.float32),
            pltpu.VMEM((ITERS, cams, rank * rank // 128, 128), jnp.float32),
            exchanged,
            exchanged,
            exchanged,
            exchanged,
            dma((cams,)),
            dma((ITERS, cams)),
            dma((ITERS, cams)),
            dma((ITERS, projs)),
            dma((ITERS, projs)),
            dma((ITERS, cams)),
            dma((ITERS, cams)),
            dma((ITERS, cams // 2)),
            dma((ITERS, cams // 2)),
            dma((ITERS, cams // 2)),
            dma((ITERS, cams // 2)),
        ],
        compiler_params=pltpu.CompilerParams(
            collective_id=0, has_side_effects=True, vmem_limit_bytes=60 * 2**20
        ),
        cost_estimate=pl.CostEstimate(
            flops=4 * ITERS * rows * columns * rank,
            bytes_accessed=2 * rows * columns,
            transcendentals=0,
        ),
    )(transport, test_panel.T)
    basis, coimage = pl.pallas_call(
        deliver,
        out_shape=results,
        in_specs=[anywhere, anywhere],
        out_specs=(anywhere, anywhere),
        scratch_shapes=[
            pltpu.VMEM((rank, rows), jnp.float32),
            pltpu.VMEM((rank, piece), jnp.float32),
            dma((4,)),
        ],
    )(basis, coimage)
    return basis.T, coimage.T


def solution(mesh):
    cams, projs = mesh.shape["cam"], mesh.shape["proj"]

    def on_device(transport, test_panel):
        if test_panel.shape[0] % 128 or transport.shape[0] % 128 or cams % 2:
            return with_collectives(transport, test_panel)
        return with_kernel(cams, projs, transport, test_panel)

    return jax.shard_map(
        on_device,
        mesh=mesh,
        in_specs=(P("cam", "proj"), P(("proj", "cam"), None)),
        out_specs=(P("cam", None), P(("proj", "cam"), None)),
        check_vma=False,
    )
```

```python
import functools

import jax
import jax.numpy as jnp
from jax import lax
from jax.experimental import pallas as pl
from jax.experimental.pallas import tpu as pltpu
from jax.sharding import PartitionSpec as P

ITERS = 2
MESH = pl.DeviceIdType.MESH
HIGHEST = lax.Precision.HIGHEST
NT = (((1,), (1,)), ((), ()))


def small_gram(block):
    return jnp.dot(block.T, block, precision=HIGHEST, preferred_element_type=jnp.float32)


def apply_factor(gram, block):
    lower = jnp.linalg.cholesky(gram)
    return jax.scipy.linalg.solve_triangular(lower, block.T, lower=True).T


def with_collectives(transport, test_panel):
    total_rows = transport.shape[0] * lax.axis_size("cam")
    panel_piece = test_panel
    for step in range(ITERS):
        partial_sketch = jnp.dot(
            transport,
            lax.all_gather(panel_piece, "cam", axis=0, tiled=True),
            preferred_element_type=jnp.float32,
        )
        sketch = lax.psum(partial_sketch, "proj")
        gram = lax.psum(small_gram(sketch), "cam") / total_rows
        basis = apply_factor(gram, sketch)
        coimage = lax.psum_scatter(
            lax.dot_general(
                transport,
                basis.astype(jnp.bfloat16),
                (((0,), (0,)), ((), ())),
                preferred_element_type=jnp.float32,
            ),
            "cam",
            scatter_dimension=0,
            tiled=True,
        )
        panel_piece = coimage.astype(jnp.bfloat16)
    return basis, coimage


def eliminate(left, right, start, stop):
    row = lax.broadcasted_iota(jnp.int32, (left.shape[0], 1), 0)
    for k in range(start, stop):
        ratio = left[:, k : k + 1] / left[k : k + 1, k : k + 1]
        ratio = jnp.where(row > k, ratio, 0.0)
        right = right - ratio * right[k : k + 1, :]
        left = left - ratio * left[k : k + 1, :]
    return left, right


def inverse_factor(left, right):
    row = lax.broadcasted_iota(jnp.int32, left.shape, 0)
    col = lax.broadcasted_iota(jnp.int32, left.shape, 1)
    pivots = jnp.sum(jnp.where(row == col, left, 0.0), axis=1, keepdims=True)
    return right / jnp.sqrt(pivots)


def kernel(
    cams,
    projs,
    transport_ref,
    panel_ref,
    basis_ref,
    coimage_ref,
    transport,
    panels,
    partials,
    grams,
    pair_out,
    pair_in,
    line_out,
    line_in,
    load_sem,
    panel_send,
    panel_recv,
    partial_send,
    partial_recv,
    gram_send,
    gram_recv,
    pair_send,
    pair_recv,
    line_send,
    line_recv,
):
    cam, proj = lax.axis_index("cam"), lax.axis_index("proj")
    rank, piece = panel_ref.shape
    rows = transport.shape[1]

    spots = cams // 2
    spot, side = cam // 2, lax.rem(cam, 2)
    other = 1 - side
    pair = 2 * spot + other
    offsets = sorted(range(1, spots), key=lambda o: -min(o, spots - o))
    line = [lax.rem(spot + o, spots) for o in offsets]
    cam_peers = [lax.rem(cam + o, cams) for o in range(1, cams)]
    proj_peers = [lax.rem(proj + o, projs) for o in range(1, projs)]

    loads = []
    for c in range(cams):
        load = pltpu.make_async_copy(
            transport_ref.at[:, pl.ds(c * piece, piece)], transport.at[c], load_sem.at[c]
        )
        load.start()
        loads.append(load)

    barrier = pltpu.get_barrier_semaphore()
    for peer in cam_peers:
        pl.semaphore_signal(barrier, inc=1, device_id=(peer, proj), device_id_type=MESH)
    for peer in proj_peers:
        pl.semaphore_signal(barrier, inc=1, device_id=(cam, peer), device_id_type=MESH)
    panels[0, cam] = panel_ref[...]
    pl.semaphore_wait(barrier, cams - 1 + projs - 1)

    def copy_of(src, dst, send_sem, recv_sem, device):
        return pltpu.make_async_remote_copy(
            src_ref=src,
            dst_ref=dst,
            send_sem=send_sem,
            recv_sem=recv_sem,
            device_id=device,
            device_id_type=MESH,
        )

    def arrived(slot, send_sem, recv_sem):
        copy_of(slot, slot, send_sem, recv_sem, (pair, proj)).wait_recv()

    folds = 128 // rank
    tall = rank // folds

    def one_pass(step, carry):
        sends = []

        def send(*parts):
            copy = copy_of(*parts)
            copy.start()
            sends.append(copy)

        def share(c, peer, sem):
            slot = panels.at[step, c]
            send(slot, slot, panel_send.at[step, sem], panel_recv.at[step, c], (peer, proj))

        def wait_panel(c):
            arrived(panels.at[step, c], panel_send.at[step, c], panel_recv.at[step, c])

        def sketched(c):
            return lax.dot_general(
                panels[step, c], transport[c], NT, preferred_element_type=jnp.float32
            )

        for s in line:
            share(cam, 2 * s + side, 2 * s + side)
        share(cam, pair, pair)

        @pl.when(step == 0)
        def _():
            for load in loads:
                load.wait()

        total = sketched(cam)
        for s in reversed(line):
            wait_panel(2 * s + side)
            share(2 * s + side, pair, 2 * s + other)
            total += sketched(2 * s + side)
        wait_panel(pair)
        total += sketched(pair)
        for s in reversed(line):
            wait_panel(2 * s + other)
            total += sketched(2 * s + other)
        partials[step, proj] = total
        for peer in proj_peers:
            slot = partials.at[step, proj]
            send(slot, slot, partial_send.at[step, peer], partial_recv.at[step, proj], (cam, peer))
        for peer in proj_peers:
            arrived(partials.at[step, peer], partial_send.at[step, peer], partial_recv.at[step, peer])
        sketch = partials[step, 0]
        for j in range(1, projs):
            sketch += partials[step, j]

        high = sketch.astype(jnp.bfloat16)
        low = (sketch - high.astype(jnp.float32)).astype(jnp.bfloat16)
        both = jnp.concatenate([high, low], axis=0)

        def product(c):
            halves = jnp.dot(both, transport[c], preferred_element_type=jnp.float32)
            return halves[:rank] + halves[rank:]

        def to_pair(s):
            pair_out[step, s] = product(2 * s + other)
            send(
                pair_out.at[step, s],
                pair_in.at[step, s],
                pair_send.at[step, s],
                pair_recv.at[step, s],
                (pair, proj),
            )

        def from_pair(s):
            arrived(pair_in.at[step, s], pair_send.at[step, s], pair_recv.at[step, s])
            return pair_in[step, s]

        to_pair(line[0])
        gram = lax.dot_general(
            sketch, sketch, NT, precision=HIGHEST, preferred_element_type=jnp.float32
        )
        grams[step, cam] = jnp.concatenate(
            [gram[f * tall : (f + 1) * tall] for f in range(folds)], axis=1
        )
        for peer in cam_peers:
            slot = grams.at[step, cam]
            send(slot, slot, gram_send.at[step, peer], gram_recv.at[step, cam], (peer, proj))
        for s in line[1:] + [spot]:
            to_pair(s)

        done = 0
        for i, s in enumerate(line):
            line_out[step, s] = product(2 * s + side) + from_pair(s)
            send(
                line_out.at[step, s],
                line_in.at[step, spot],
                line_send.at[step, s],
                line_recv.at[step, spot],
                (2 * s + side, proj),
            )
            if i == 0:
                for peer in cam_peers:
                    arrived(grams.at[step, peer], gram_send.at[step, peer], gram_recv.at[step, peer])
                folded = grams[step, 0]
                for c in range(1, cams):
                    folded += grams[step, c]
                folded = folded / (rows * cams)
                left = jnp.concatenate(
                    [folded[:, f * rank : (f + 1) * rank] for f in range(folds)], axis=0
                )
                row = lax.broadcasted_iota(jnp.int32, (rank, rank), 0)
                col = lax.broadcasted_iota(jnp.int32, (rank, rank), 1)
                right = jnp.where(row == col, 1.0, 0.0).astype(jnp.float32)
            upto = rank * (i + 1) // len(line)
            left, right = eliminate(left, right, done, upto)
            done = upto
        inverse = inverse_factor(left, right)
        summed = product(cam) + from_pair(spot)
        basis_ref[...] = jnp.dot(
            inverse, sketch, precision=HIGHEST, preferred_element_type=jnp.float32
        )

        for s in reversed(line):
            arrived(line_in.at[step, s], line_send.at[step, s], line_recv.at[step, s])
            summed += line_in[step, s]
        coimage = jnp.dot(inverse, summed, precision=HIGHEST, preferred_element_type=jnp.float32)
        coimage_ref[...] = coimage
        panels[step + 1, cam] = coimage.astype(jnp.bfloat16)
        for copy in sends:
            copy.wait_send()
        return carry

    lax.fori_loop(0, ITERS, one_pass, 0)


def deliver(basis_ref, coimage_ref, basis_out, coimage_out, basis, coimage, sem):
    reads = [
        pltpu.make_async_copy(basis_ref, basis, sem.at[0]),
        pltpu.make_async_copy(coimage_ref, coimage, sem.at[1]),
    ]
    writes = [
        pltpu.make_async_copy(basis, basis_out, sem.at[2]),
        pltpu.make_async_copy(coimage, coimage_out, sem.at[3]),
    ]
    for read in reads:
        read.start()
    for read, write in zip(reads, writes):
        read.wait()
        write.start()
    for write in writes:
        write.wait()


def with_kernel(cams, projs, transport, test_panel):
    rows, columns = transport.shape
    piece, rank = test_panel.shape
    dma = pltpu.SemaphoreType.DMA
    in_vmem = pl.BlockSpec(memory_space=pltpu.VMEM)
    anywhere = pl.BlockSpec(memory_space=pl.ANY)
    results = (
        jax.ShapeDtypeStruct((rank, rows), jnp.float32),
        jax.ShapeDtypeStruct((rank, piece), jnp.float32),
    )
    exchanged = pltpu.VMEM((ITERS, cams // 2, rank, piece), jnp.float32)
    basis, coimage = pl.pallas_call(
        functools.partial(kernel, cams, projs),
        out_shape=results,
        in_specs=[anywhere, in_vmem],
        out_specs=(in_vmem, in_vmem),
        scratch_shapes=[
            pltpu.VMEM((cams, rows, piece), jnp.bfloat16),
            pltpu.VMEM((ITERS + 1, cams, rank, piece), jnp.bfloat16),
            pltpu.VMEM((ITERS, projs, rank, rows), jnp.float32),
            pltpu.VMEM((ITERS, cams, rank * rank // 128, 128), jnp.float32),
            exchanged,
            exchanged,
            exchanged,
            exchanged,
            dma((cams,)),
            dma((ITERS, cams)),
            dma((ITERS, cams)),
            dma((ITERS, projs)),
            dma((ITERS, projs)),
            dma((ITERS, cams)),
            dma((ITERS, cams)),
            dma((ITERS, cams // 2)),
            dma((ITERS, cams // 2)),
            dma((ITERS, cams // 2)),
            dma((ITERS, cams // 2)),
        ],
        compiler_params=pltpu.CompilerParams(
            collective_id=0, has_side_effects=True, vmem_limit_bytes=60 * 2**20
        ),
        cost_estimate=pl.CostEstimate(
            flops=4 * ITERS * rows * columns * rank,
            bytes_accessed=2 * rows * columns,
            transcendentals=0,
        ),
    )(transport, test_panel.T)
    basis, coimage = pl.pallas_call(
        deliver,
        out_shape=results,
        in_specs=[anywhere, anywhere],
        out_specs=(anywhere, anywhere),
        scratch_shapes=[
            pltpu.VMEM((rank, rows), jnp.float32),
            pltpu.VMEM((rank, piece), jnp.float32),
            dma((4,)),
        ],
    )(basis, coimage)
    return basis.T, coimage.T


def solution(mesh):
    cams, projs = mesh.shape["cam"], mesh.shape["proj"]

    def on_device(transport, test_panel):
        if test_panel.shape[0] % 128 or transport.shape[0] % 128 or cams % 2 or cams < 4:
            return with_collectives(transport, test_panel)
        return with_kernel(cams, projs, transport, test_panel)

    return jax.shard_map(
        on_device,
        mesh=mesh,
        in_specs=(P("cam", "proj"), P(("proj", "cam"), None)),
        out_specs=(P("cam", None), P(("proj", "cam"), None)),
        check_vma=False,
    )
```

```python
import functools

import jax
import jax.numpy as jnp
from jax import lax
from jax.experimental import pallas as pl
from jax.experimental.pallas import tpu as pltpu
from jax.sharding import PartitionSpec as P

ITERS = 2
MESH = pl.DeviceIdType.MESH
HIGHEST = lax.Precision.HIGHEST
NT = (((1,), (1,)), ((), ()))


def small_gram(block):
    return jnp.dot(block.T, block, precision=HIGHEST, preferred_element_type=jnp.float32)


def apply_factor(gram, block):
    lower = jnp.linalg.cholesky(gram)
    return jax.scipy.linalg.solve_triangular(lower, block.T, lower=True).T


def with_collectives(transport, test_panel):
    total_rows = transport.shape[0] * lax.axis_size("cam")
    panel_piece = test_panel
    for step in range(ITERS):
        partial_sketch = jnp.dot(
            transport,
            lax.all_gather(panel_piece, "cam", axis=0, tiled=True),
            preferred_element_type=jnp.float32,
        )
        sketch = lax.psum(partial_sketch, "proj")
        gram = lax.psum(small_gram(sketch), "cam") / total_rows
        basis = apply_factor(gram, sketch)
        coimage = lax.psum_scatter(
            lax.dot_general(
                transport,
                basis.astype(jnp.bfloat16),
                (((0,), (0,)), ((), ())),
                preferred_element_type=jnp.float32,
            ),
            "cam",
            scatter_dimension=0,
            tiled=True,
        )
        panel_piece = coimage.astype(jnp.bfloat16)
    return basis, coimage


def eliminate(left, right, start, stop):
    row = lax.broadcasted_iota(jnp.int32, (left.shape[0], 1), 0)
    for k in range(start, stop):
        ratio = left[:, k : k + 1] / left[k : k + 1, k : k + 1]
        ratio = jnp.where(row > k, ratio, 0.0)
        right = right - ratio * right[k : k + 1, :]
        left = left - ratio * left[k : k + 1, :]
    return left, right


def inverse_factor(left, right):
    row = lax.broadcasted_iota(jnp.int32, left.shape, 0)
    col = lax.broadcasted_iota(jnp.int32, left.shape, 1)
    pivots = jnp.sum(jnp.where(row == col, left, 0.0), axis=1, keepdims=True)
    return right / jnp.sqrt(pivots)


def kernel(
    cams,
    projs,
    transport_ref,
    panel_ref,
    basis_ref,
    coimage_ref,
    transport,
    panels,
    partials,
    duos,
    grams,
    pair_out,
    pair_in,
    line_out,
    line_in,
    load_sem,
    panel_send,
    panel_recv,
    partial_send,
    partial_recv,
    duo_send,
    duo_recv,
    gram_send,
    gram_recv,
    pair_send,
    pair_recv,
    line_send,
    line_recv,
):
    cam, proj = lax.axis_index("cam"), lax.axis_index("proj")
    rank, piece = panel_ref.shape
    rows = transport.shape[1]

    spots = cams // 2
    spot, side = cam // 2, lax.rem(cam, 2)
    other = 1 - side
    pair = 2 * spot + other
    offsets = sorted(range(1, spots), key=lambda o: -min(o, spots - o))
    line = [lax.rem(spot + o, spots) for o in offsets]
    cam_peers = [lax.rem(cam + o, cams) for o in range(1, cams)]
    duo, core = proj // 2, lax.rem(proj, 2)
    sibling = 2 * duo + 1 - core
    other_duos = [lax.rem(duo + o, projs // 2) for o in range(1, projs // 2)]
    proj_peers = [sibling] + [2 * d + core for d in other_duos]

    loads = []
    for c in range(cams):
        load = pltpu.make_async_copy(
            transport_ref.at[:, pl.ds(c * piece, piece)], transport.at[c], load_sem.at[c]
        )
        load.start()
        loads.append(load)

    barrier = pltpu.get_barrier_semaphore()
    for peer in cam_peers:
        pl.semaphore_signal(barrier, inc=1, device_id=(peer, proj), device_id_type=MESH)
    for peer in proj_peers:
        pl.semaphore_signal(barrier, inc=1, device_id=(cam, peer), device_id_type=MESH)
    panels[0, cam] = panel_ref[...]
    pl.semaphore_wait(barrier, cams - 1 + projs // 2)

    def copy_of(src, dst, send_sem, recv_sem, device):
        return pltpu.make_async_remote_copy(
            src_ref=src,
            dst_ref=dst,
            send_sem=send_sem,
            recv_sem=recv_sem,
            device_id=device,
            device_id_type=MESH,
        )

    def arrived(slot, send_sem, recv_sem):
        copy_of(slot, slot, send_sem, recv_sem, (pair, proj)).wait_recv()

    folds = 128 // rank
    tall = rank // folds

    def one_pass(step, carry):
        sends = []

        def send(*parts):
            copy = copy_of(*parts)
            copy.start()
            sends.append(copy)

        def share(c, peer, sem):
            slot = panels.at[step, c]
            send(slot, slot, panel_send.at[step, sem], panel_recv.at[step, c], (peer, proj))

        def wait_panel(c):
            arrived(panels.at[step, c], panel_send.at[step, c], panel_recv.at[step, c])

        def sketched(c):
            return lax.dot_general(
                panels[step, c], transport[c], NT, preferred_element_type=jnp.float32
            )

        for s in line:
            share(cam, 2 * s + side, 2 * s + side)
        share(cam, pair, pair)

        @pl.when(step == 0)
        def _():
            for load in loads:
                load.wait()

        total = sketched(cam)
        for s in reversed(line):
            wait_panel(2 * s + side)
            share(2 * s + side, pair, 2 * s + other)
            total += sketched(2 * s + side)
        wait_panel(pair)
        total += sketched(pair)
        for s in reversed(line):
            wait_panel(2 * s + other)
            total += sketched(2 * s + other)
        partials[step, core] = total
        slot = partials.at[step, core]
        send(slot, slot, partial_send.at[step, 0], partial_recv.at[step, 0], (cam, sibling))
        arrived(partials.at[step, 1 - core], partial_send.at[step, 0], partial_recv.at[step, 0])
        duos[step, duo] = partials[step, 0] + partials[step, 1]
        for d in other_duos:
            slot = duos.at[step, duo]
            send(slot, slot, duo_send.at[step, d], duo_recv.at[step, duo], (cam, 2 * d + core))
        for d in other_duos:
            arrived(duos.at[step, d], duo_send.at[step, d], duo_recv.at[step, d])
        sketch = duos[step, 0]
        for d in range(1, projs // 2):
            sketch += duos[step, d]

        high = sketch.astype(jnp.bfloat16)
        low = (sketch - high.astype(jnp.float32)).astype(jnp.bfloat16)
        both = jnp.concatenate([high, low], axis=0)

        def product(c):
            halves = jnp.dot(both, transport[c], preferred_element_type=jnp.float32)
            return halves[:rank] + halves[rank:]

        def to_pair(s):
            pair_out[step, s] = product(2 * s + other)
            send(
                pair_out.at[step, s],
                pair_in.at[step, s],
                pair_send.at[step, s],
                pair_recv.at[step, s],
                (pair, proj),
            )

        def from_pair(s):
            arrived(pair_in.at[step, s], pair_send.at[step, s], pair_recv.at[step, s])
            return pair_in[step, s]

        to_pair(line[0])
        gram = lax.dot_general(
            sketch, sketch, NT, precision=HIGHEST, preferred_element_type=jnp.float32
        )
        grams[step, cam] = jnp.concatenate(
            [gram[f * tall : (f + 1) * tall] for f in range(folds)], axis=1
        )
        for peer in cam_peers:
            slot = grams.at[step, cam]
            send(slot, slot, gram_send.at[step, peer], gram_recv.at[step, cam], (peer, proj))
        for s in line[1:] + [spot]:
            to_pair(s)

        for s in line:
            line_out[step, s] = product(2 * s + side) + from_pair(s)
            send(
                line_out.at[step, s],
                line_in.at[step, spot],
                line_send.at[step, s],
                line_recv.at[step, spot],
                (2 * s + side, proj),
            )
        for peer in cam_peers:
            arrived(grams.at[step, peer], gram_send.at[step, peer], gram_recv.at[step, peer])
        folded = grams[step, 0]
        for c in range(1, cams):
            folded += grams[step, c]
        folded = folded / (rows * cams)
        left = jnp.concatenate(
            [folded[:, f * rank : (f + 1) * rank] for f in range(folds)], axis=0
        )
        row = lax.broadcasted_iota(jnp.int32, (rank, rank), 0)
        col = lax.broadcasted_iota(jnp.int32, (rank, rank), 1)
        identity = jnp.where(row == col, 1.0, 0.0).astype(jnp.float32)
        left, right = eliminate(left, identity, 0, rank)
        inverse = inverse_factor(left, right)
        summed = product(cam) + from_pair(spot)
        basis_ref[...] = jnp.dot(
            inverse, sketch, precision=HIGHEST, preferred_element_type=jnp.float32
        )

        for s in reversed(line):
            arrived(line_in.at[step, s], line_send.at[step, s], line_recv.at[step, s])
            summed += line_in[step, s]
        coimage = jnp.dot(inverse, summed, precision=HIGHEST, preferred_element_type=jnp.float32)
        coimage_ref[...] = coimage
        panels[step + 1, cam] = coimage.astype(jnp.bfloat16)
        for copy in sends:
            copy.wait_send()
        return carry

    lax.fori_loop(0, ITERS, one_pass, 0)


def deliver(basis_ref, coimage_ref, basis_out, coimage_out, basis, coimage, sem):
    reads = [
        pltpu.make_async_copy(basis_ref, basis, sem.at[0]),
        pltpu.make_async_copy(coimage_ref, coimage, sem.at[1]),
    ]
    writes = [
        pltpu.make_async_copy(basis, basis_out, sem.at[2]),
        pltpu.make_async_copy(coimage, coimage_out, sem.at[3]),
    ]
    for read in reads:
        read.start()
    for read, write in zip(reads, writes):
        read.wait()
        write.start()
    for write in writes:
        write.wait()


def with_kernel(cams, projs, transport, test_panel):
    rows, columns = transport.shape
    piece, rank = test_panel.shape
    dma = pltpu.SemaphoreType.DMA
    in_vmem = pl.BlockSpec(memory_space=pltpu.VMEM)
    anywhere = pl.BlockSpec(memory_space=pl.ANY)
    results = (
        jax.ShapeDtypeStruct((rank, rows), jnp.float32),
        jax.ShapeDtypeStruct((rank, piece), jnp.float32),
    )
    exchanged = pltpu.VMEM((ITERS, cams // 2, rank, piece), jnp.float32)
    basis, coimage = pl.pallas_call(
        functools.partial(kernel, cams, projs),
        out_shape=results,
        in_specs=[anywhere, in_vmem],
        out_specs=(in_vmem, in_vmem),
        scratch_shapes=[
            pltpu.VMEM((cams, rows, piece), jnp.bfloat16),
            pltpu.VMEM((ITERS + 1, cams, rank, piece), jnp.bfloat16),
            pltpu.VMEM((ITERS, 2, rank, rows), jnp.float32),
            pltpu.VMEM((ITERS, projs // 2, rank, rows), jnp.float32),
            pltpu.VMEM((ITERS, cams, rank * rank // 128, 128), jnp.float32),
            exchanged,
            exchanged,
            exchanged,
            exchanged,
            dma((cams,)),
            dma((ITERS, cams)),
            dma((ITERS, cams)),
            dma((ITERS, 1)),
            dma((ITERS, 1)),
            dma((ITERS, projs // 2)),
            dma((ITERS, projs // 2)),
            dma((ITERS, cams)),
            dma((ITERS, cams)),
            dma((ITERS, cams // 2)),
            dma((ITERS, cams // 2)),
            dma((ITERS, cams // 2)),
            dma((ITERS, cams // 2)),
        ],
        compiler_params=pltpu.CompilerParams(
            collective_id=0, has_side_effects=True, vmem_limit_bytes=60 * 2**20
        ),
        cost_estimate=pl.CostEstimate(
            flops=4 * ITERS * rows * columns * rank,
            bytes_accessed=2 * rows * columns,
            transcendentals=0,
        ),
    )(transport, test_panel.T)
    basis, coimage = pl.pallas_call(
        deliver,
        out_shape=results,
        in_specs=[anywhere, anywhere],
        out_specs=(anywhere, anywhere),
        scratch_shapes=[
            pltpu.VMEM((rank, rows), jnp.float32),
            pltpu.VMEM((rank, piece), jnp.float32),
            dma((4,)),
        ],
    )(basis, coimage)
    return basis.T, coimage.T


def solution(mesh):
    cams, projs = mesh.shape["cam"], mesh.shape["proj"]

    def on_device(transport, test_panel):
        if test_panel.shape[0] % 128 or transport.shape[0] % 128 or cams % 2 or projs % 2:
            return with_collectives(transport, test_panel)
        return with_kernel(cams, projs, transport, test_panel)

    return jax.shard_map(
        on_device,
        mesh=mesh,
        in_specs=(P("cam", "proj"), P(("proj", "cam"), None)),
        out_specs=(P("cam", None), P(("proj", "cam"), None)),
        check_vma=False,
    )
```

```python
import functools

import jax
import jax.numpy as jnp
from jax import lax
from jax.experimental import pallas as pl
from jax.experimental.pallas import tpu as pltpu
from jax.sharding import PartitionSpec as P

ITERS = 2
MESH = pl.DeviceIdType.MESH
HIGHEST = lax.Precision.HIGHEST
NT = (((1,), (1,)), ((), ()))


def small_gram(block):
    return jnp.dot(block.T, block, precision=HIGHEST, preferred_element_type=jnp.float32)


def apply_factor(gram, block):
    lower = jnp.linalg.cholesky(gram)
    return jax.scipy.linalg.solve_triangular(lower, block.T, lower=True).T


def with_collectives(transport, test_panel):
    total_rows = transport.shape[0] * lax.axis_size("cam")
    panel_piece = test_panel
    for step in range(ITERS):
        partial_sketch = jnp.dot(
            transport,
            lax.all_gather(panel_piece, "cam", axis=0, tiled=True),
            preferred_element_type=jnp.float32,
        )
        sketch = lax.psum(partial_sketch, "proj")
        gram = lax.psum(small_gram(sketch), "cam") / total_rows
        basis = apply_factor(gram, sketch)
        coimage = lax.psum_scatter(
            lax.dot_general(
                transport,
                basis.astype(jnp.bfloat16),
                (((0,), (0,)), ((), ())),
                preferred_element_type=jnp.float32,
            ),
            "cam",
            scatter_dimension=0,
            tiled=True,
        )
        panel_piece = coimage.astype(jnp.bfloat16)
    return basis, coimage


def eliminate(left, right, start, stop):
    row = lax.broadcasted_iota(jnp.int32, (left.shape[0], 1), 0)
    for k in range(start, stop):
        ratio = left[:, k : k + 1] / left[k : k + 1, k : k + 1]
        ratio = jnp.where(row > k, ratio, 0.0)
        right = right - ratio * right[k : k + 1, :]
        left = left - ratio * left[k : k + 1, :]
    return left, right


def inverse_factor(left, right):
    row = lax.broadcasted_iota(jnp.int32, left.shape, 0)
    col = lax.broadcasted_iota(jnp.int32, left.shape, 1)
    pivots = jnp.sum(jnp.where(row == col, left, 0.0), axis=1, keepdims=True)
    return right / jnp.sqrt(pivots)


def kernel(
    cams,
    projs,
    transport_ref,
    panel_ref,
    basis_ref,
    coimage_ref,
    transport,
    panels,
    partials,
    duos,
    grams,
    pair_out,
    pair_in,
    line_out,
    line_in,
    load_sem,
    panel_send,
    panel_recv,
    partial_send,
    partial_recv,
    duo_send,
    duo_recv,
    gram_send,
    gram_recv,
    pair_send,
    pair_recv,
    line_send,
    line_recv,
):
    cam, proj = lax.axis_index("cam"), lax.axis_index("proj")
    rank, piece = panel_ref.shape
    rows = transport.shape[1]

    spots = cams // 2
    spot, side = cam // 2, lax.rem(cam, 2)
    other = 1 - side
    pair = 2 * spot + other
    offsets = sorted(range(1, spots), key=lambda o: -min(o, spots - o))
    line = [lax.rem(spot + o, spots) for o in offsets]
    cam_peers = [lax.rem(cam + o, cams) for o in range(1, cams)]
    duo, core = proj // 2, lax.rem(proj, 2)
    sibling = 2 * duo + 1 - core
    other_duos = [lax.rem(duo + o, projs // 2) for o in range(1, projs // 2)]
    proj_peers = [sibling] + [2 * d + core for d in other_duos]

    loads = []
    for c in range(cams):
        load = pltpu.make_async_copy(
            transport_ref.at[:, pl.ds(c * piece, piece)], transport.at[c], load_sem.at[c]
        )
        load.start()
        loads.append(load)

    barrier = pltpu.get_barrier_semaphore()
    for peer in cam_peers:
        pl.semaphore_signal(barrier, inc=1, device_id=(peer, proj), device_id_type=MESH)
    for peer in proj_peers:
        pl.semaphore_signal(barrier, inc=1, device_id=(cam, peer), device_id_type=MESH)
    panels[0, cam] = panel_ref[...]
    pl.semaphore_wait(barrier, cams - 1 + projs // 2)

    def copy_of(src, dst, send_sem, recv_sem, device):
        return pltpu.make_async_remote_copy(
            src_ref=src,
            dst_ref=dst,
            send_sem=send_sem,
            recv_sem=recv_sem,
            device_id=device,
            device_id_type=MESH,
        )

    def arrived(slot, send_sem, recv_sem):
        copy_of(slot, slot, send_sem, recv_sem, (pair, proj)).wait_recv()

    folds = 128 // rank
    tall = rank // folds

    def one_pass(step, carry):
        sends = []

        def send(*parts):
            copy = copy_of(*parts)
            copy.start()
            sends.append(copy)

        def share(c, peer, sem):
            slot = panels.at[step, c]
            send(slot, slot, panel_send.at[step, sem], panel_recv.at[step, c], (peer, proj))

        def wait_panel(c):
            arrived(panels.at[step, c], panel_send.at[step, c], panel_recv.at[step, c])

        def sketched(c):
            return lax.dot_general(
                panels[step, c], transport[c], NT, preferred_element_type=jnp.float32
            )

        for s in line:
            share(cam, 2 * s + side, 2 * s + side)
        share(cam, pair, pair)

        @pl.when(step == 0)
        def _():
            for load in loads:
                load.wait()

        total = sketched(cam)
        for s in reversed(line):
            wait_panel(2 * s + side)
            share(2 * s + side, pair, 2 * s + other)
            total += sketched(2 * s + side)
        wait_panel(pair)
        total += sketched(pair)
        for s in reversed(line):
            wait_panel(2 * s + other)
            total += sketched(2 * s + other)
        partials[step, core] = total
        slot = partials.at[step, core]
        send(slot, slot, partial_send.at[step, 0], partial_recv.at[step, 0], (cam, sibling))
        arrived(partials.at[step, 1 - core], partial_send.at[step, 0], partial_recv.at[step, 0])
        duos[step, duo] = partials[step, 0] + partials[step, 1]
        for d in other_duos:
            slot = duos.at[step, duo]
            send(slot, slot, duo_send.at[step, d], duo_recv.at[step, duo], (cam, 2 * d + core))
        for d in other_duos:
            arrived(duos.at[step, d], duo_send.at[step, d], duo_recv.at[step, d])
        sketch = duos[step, 0]
        for d in range(1, projs // 2):
            sketch += duos[step, d]

        high = sketch.astype(jnp.bfloat16)
        low = (sketch - high.astype(jnp.float32)).astype(jnp.bfloat16)
        both = jnp.concatenate([high, low], axis=0)

        def product(c):
            halves = jnp.dot(both, transport[c], preferred_element_type=jnp.float32)
            return halves[:rank] + halves[rank:]

        def to_pair(s):
            pair_out[step, s] = product(2 * s + other)
            send(
                pair_out.at[step, s],
                pair_in.at[step, s],
                pair_send.at[step, s],
                pair_recv.at[step, s],
                (pair, proj),
            )

        def from_pair(s):
            arrived(pair_in.at[step, s], pair_send.at[step, s], pair_recv.at[step, s])
            return pair_in[step, s]

        to_pair(line[0])
        gram = lax.dot_general(
            sketch, sketch, NT, precision=HIGHEST, preferred_element_type=jnp.float32
        )
        grams[step, cam] = jnp.concatenate(
            [gram[f * tall : (f + 1) * tall] for f in range(folds)], axis=1
        )
        for peer in cam_peers:
            slot = grams.at[step, cam]
            send(slot, slot, gram_send.at[step, peer], gram_recv.at[step, cam], (peer, proj))
        for s in line[1:] + [spot]:
            to_pair(s)

        for s in line:
            line_out[step, s] = product(2 * s + side) + from_pair(s)
            send(
                line_out.at[step, s],
                line_in.at[step, spot],
                line_send.at[step, s],
                line_recv.at[step, spot],
                (2 * s + side, proj),
            )
        for peer in cam_peers:
            arrived(grams.at[step, peer], gram_send.at[step, peer], gram_recv.at[step, peer])
        folded = grams[step, 0]
        for c in range(1, cams):
            folded += grams[step, c]
        folded = folded / (rows * cams)
        left = jnp.concatenate(
            [folded[:, f * rank : (f + 1) * rank] for f in range(folds)], axis=0
        )
        row = lax.broadcasted_iota(jnp.int32, (rank, rank), 0)
        col = lax.broadcasted_iota(jnp.int32, (rank, rank), 1)
        identity = jnp.where(row == col, 1.0, 0.0).astype(jnp.float32)
        left, right = eliminate(left, identity, 0, rank)
        inverse = inverse_factor(left, right)
        summed = product(cam) + from_pair(spot)
        basis_ref[...] = jnp.dot(
            inverse, sketch, precision=HIGHEST, preferred_element_type=jnp.float32
        )

        for s in reversed(line):
            arrived(line_in.at[step, s], line_send.at[step, s], line_recv.at[step, s])
            summed += line_in[step, s]
        coimage = jnp.dot(inverse, summed, precision=HIGHEST, preferred_element_type=jnp.float32)
        coimage_ref[...] = coimage
        panels[step + 1, cam] = coimage.astype(jnp.bfloat16)
        for copy in sends:
            copy.wait_send()
        return carry

    lax.fori_loop(0, ITERS, one_pass, 0)


def deliver(basis_ref, coimage_ref, basis_out, coimage_out, sem):
    writes = [
        pltpu.make_async_copy(basis_ref, basis_out, sem.at[0]),
        pltpu.make_async_copy(coimage_ref, coimage_out, sem.at[1]),
    ]
    for write in writes:
        write.start()
    for write in writes:
        write.wait()


def with_kernel(cams, projs, transport, test_panel):
    rows, columns = transport.shape
    piece, rank = test_panel.shape
    dma = pltpu.SemaphoreType.DMA
    in_vmem = pl.BlockSpec(memory_space=pltpu.VMEM)
    anywhere = pl.BlockSpec(memory_space=pl.ANY)
    results = (
        jax.ShapeDtypeStruct((rank, rows), jnp.float32),
        jax.ShapeDtypeStruct((rank, piece), jnp.float32),
    )
    kept = (pltpu.VMEM((rank, rows), jnp.float32), pltpu.VMEM((rank, piece), jnp.float32))
    exchanged = pltpu.VMEM((ITERS, cams // 2, rank, piece), jnp.float32)
    basis, coimage = pl.pallas_call(
        functools.partial(kernel, cams, projs),
        out_shape=kept,
        in_specs=[anywhere, in_vmem],
        out_specs=(in_vmem, in_vmem),
        scratch_shapes=[
            pltpu.VMEM((cams, rows, piece), jnp.bfloat16),
            pltpu.VMEM((ITERS + 1, cams, rank, piece), jnp.bfloat16),
            pltpu.VMEM((ITERS, 2, rank, rows), jnp.float32),
            pltpu.VMEM((ITERS, projs // 2, rank, rows), jnp.float32),
            pltpu.VMEM((ITERS, cams, rank * rank // 128, 128), jnp.float32),
            exchanged,
            exchanged,
            exchanged,
            exchanged,
            dma((cams,)),
            dma((ITERS, cams)),
            dma((ITERS, cams)),
            dma((ITERS, 1)),
            dma((ITERS, 1)),
            dma((ITERS, projs // 2)),
            dma((ITERS, projs // 2)),
            dma((ITERS, cams)),
            dma((ITERS, cams)),
            dma((ITERS, cams // 2)),
            dma((ITERS, cams // 2)),
            dma((ITERS, cams // 2)),
            dma((ITERS, cams // 2)),
        ],
        compiler_params=pltpu.CompilerParams(
            collective_id=0, has_side_effects=True, vmem_limit_bytes=60 * 2**20
        ),
        cost_estimate=pl.CostEstimate(
            flops=4 * ITERS * rows * columns * rank,
            bytes_accessed=2 * rows * columns,
            transcendentals=0,
        ),
    )(transport, test_panel.T)
    basis, coimage = pl.pallas_call(
        deliver,
        out_shape=results,
        in_specs=[in_vmem, in_vmem],
        out_specs=(anywhere, anywhere),
        scratch_shapes=[dma((2,))],
    )(basis, coimage)
    return basis.T, coimage.T


def solution(mesh):
    cams, projs = mesh.shape["cam"], mesh.shape["proj"]

    def on_device(transport, test_panel):
        if test_panel.shape[0] % 128 or transport.shape[0] % 128 or cams % 2 or projs % 2:
            return with_collectives(transport, test_panel)
        return with_kernel(cams, projs, transport, test_panel)

    return jax.shard_map(
        on_device,
        mesh=mesh,
        in_specs=(P("cam", "proj"), P(("proj", "cam"), None)),
        out_specs=(P("cam", None), P(("proj", "cam"), None)),
        check_vma=False,
    )
```

```python
import functools

import jax
import jax.numpy as jnp
from jax import lax
from jax.experimental import pallas as pl
from jax.experimental.pallas import tpu as pltpu
from jax.sharding import PartitionSpec as P

ITERS = 2
CUTS = 2
MESH = pl.DeviceIdType.MESH
HIGHEST = lax.Precision.HIGHEST
NT = (((1,), (1,)), ((), ()))


def small_gram(block):
    return jnp.dot(block.T, block, precision=HIGHEST, preferred_element_type=jnp.float32)


def apply_factor(gram, block):
    lower = jnp.linalg.cholesky(gram)
    return jax.scipy.linalg.solve_triangular(lower, block.T, lower=True).T


def with_collectives(transport, test_panel):
    total_rows = transport.shape[0] * lax.axis_size("cam")
    panel_piece = test_panel
    for step in range(ITERS):
        partial_sketch = jnp.dot(
            transport,
            lax.all_gather(panel_piece, "cam", axis=0, tiled=True),
            preferred_element_type=jnp.float32,
        )
        sketch = lax.psum(partial_sketch, "proj")
        gram = lax.psum(small_gram(sketch), "cam") / total_rows
        basis = apply_factor(gram, sketch)
        coimage = lax.psum_scatter(
            lax.dot_general(
                transport,
                basis.astype(jnp.bfloat16),
                (((0,), (0,)), ((), ())),
                preferred_element_type=jnp.float32,
            ),
            "cam",
            scatter_dimension=0,
            tiled=True,
        )
        panel_piece = coimage.astype(jnp.bfloat16)
    return basis, coimage


def eliminate(left, right, start, stop):
    row = lax.broadcasted_iota(jnp.int32, (left.shape[0], 1), 0)
    for k in range(start, stop):
        ratio = left[:, k : k + 1] / left[k : k + 1, k : k + 1]
        ratio = jnp.where(row > k, ratio, 0.0)
        right = right - ratio * right[k : k + 1, :]
        left = left - ratio * left[k : k + 1, :]
    return left, right


def inverse_factor(left, right):
    row = lax.broadcasted_iota(jnp.int32, left.shape, 0)
    col = lax.broadcasted_iota(jnp.int32, left.shape, 1)
    pivots = jnp.sum(jnp.where(row == col, left, 0.0), axis=1, keepdims=True)
    return right / jnp.sqrt(pivots)


def kernel(
    cams,
    projs,
    transport_ref,
    panel_ref,
    basis_ref,
    coimage_ref,
    transport,
    panels,
    partials,
    duos,
    grams,
    pair_out,
    pair_in,
    line_out,
    line_in,
    load_sem,
    panel_send,
    panel_recv,
    partial_send,
    partial_recv,
    duo_send,
    duo_recv,
    gram_send,
    gram_recv,
    pair_send,
    pair_recv,
    line_send,
    line_recv,
):
    cam, proj = lax.axis_index("cam"), lax.axis_index("proj")
    rank, piece = panel_ref.shape
    rows = transport.shape[1]
    width = piece // CUTS

    spots = cams // 2
    spot, side = cam // 2, lax.rem(cam, 2)
    other = 1 - side
    pair = 2 * spot + other
    offsets = sorted(range(1, spots), key=lambda o: -min(o, spots - o))
    line = [lax.rem(spot + o, spots) for o in offsets]
    cam_peers = [lax.rem(cam + o, cams) for o in range(1, cams)]
    duo, core = proj // 2, lax.rem(proj, 2)
    sibling = 2 * duo + 1 - core
    other_duos = [lax.rem(duo + o, projs // 2) for o in range(1, projs // 2)]
    proj_peers = [sibling] + [2 * d + core for d in other_duos]

    loads = []
    for c in range(cams):
        load = pltpu.make_async_copy(
            transport_ref.at[:, pl.ds(c * piece, piece)], transport.at[c], load_sem.at[c]
        )
        load.start()
        loads.append(load)

    barrier = pltpu.get_barrier_semaphore()
    for peer in cam_peers:
        pl.semaphore_signal(barrier, inc=1, device_id=(peer, proj), device_id_type=MESH)
    for peer in proj_peers:
        pl.semaphore_signal(barrier, inc=1, device_id=(cam, peer), device_id_type=MESH)
    panels[0, cam] = panel_ref[...]
    pl.semaphore_wait(barrier, cams - 1 + projs // 2)

    def copy_of(src, dst, send_sem, recv_sem, device):
        return pltpu.make_async_remote_copy(
            src_ref=src,
            dst_ref=dst,
            send_sem=send_sem,
            recv_sem=recv_sem,
            device_id=device,
            device_id_type=MESH,
        )

    def arrived(slot, send_sem, recv_sem):
        copy_of(slot, slot, send_sem, recv_sem, (pair, proj)).wait_recv()

    folds = 128 // rank
    tall = rank // folds

    def one_pass(step, carry):
        sends = []

        def send(*parts):
            copy = copy_of(*parts)
            copy.start()
            sends.append(copy)

        def share(c, peer, sem):
            slot = panels.at[step, c]
            send(slot, slot, panel_send.at[step, sem], panel_recv.at[step, c], (peer, proj))

        def wait_panel(c):
            arrived(panels.at[step, c], panel_send.at[step, c], panel_recv.at[step, c])

        def sketched(c):
            return lax.dot_general(
                panels[step, c], transport[c], NT, preferred_element_type=jnp.float32
            )

        for s in line:
            share(cam, 2 * s + side, 2 * s + side)
        share(cam, pair, pair)

        @pl.when(step == 0)
        def _():
            for load in loads:
                load.wait()

        total = sketched(cam)
        for s in reversed(line):
            wait_panel(2 * s + side)
            share(2 * s + side, pair, 2 * s + other)
            total += sketched(2 * s + side)
        wait_panel(pair)
        total += sketched(pair)
        for s in reversed(line):
            wait_panel(2 * s + other)
            total += sketched(2 * s + other)
        partials[step, core] = total
        slot = partials.at[step, core]
        send(slot, slot, partial_send.at[step, 0], partial_recv.at[step, 0], (cam, sibling))
        arrived(partials.at[step, 1 - core], partial_send.at[step, 0], partial_recv.at[step, 0])
        duos[step, duo] = partials[step, 0] + partials[step, 1]
        for d in other_duos:
            slot = duos.at[step, duo]
            send(slot, slot, duo_send.at[step, d], duo_recv.at[step, duo], (cam, 2 * d + core))
        for d in other_duos:
            arrived(duos.at[step, d], duo_send.at[step, d], duo_recv.at[step, d])
        sketch = duos[step, 0]
        for d in range(1, projs // 2):
            sketch += duos[step, d]

        high = sketch.astype(jnp.bfloat16)
        low = (sketch - high.astype(jnp.float32)).astype(jnp.bfloat16)
        both = jnp.concatenate([high, low], axis=0)

        def product(c, h):
            block = transport[c, :, h * width : (h + 1) * width]
            halves = jnp.dot(both, block, preferred_element_type=jnp.float32)
            return halves[:rank] + halves[rank:]

        def to_pair(s):
            for h in range(CUTS):
                pair_out[step, s, h] = product(2 * s + other, h)
                send(
                    pair_out.at[step, s, h],
                    pair_in.at[step, s, h],
                    pair_send.at[step, s, h],
                    pair_recv.at[step, s, h],
                    (pair, proj),
                )

        def from_pair(s, h):
            arrived(pair_in.at[step, s, h], pair_send.at[step, s, h], pair_recv.at[step, s, h])
            return pair_in[step, s, h]

        to_pair(line[0])
        gram = lax.dot_general(
            sketch, sketch, NT, precision=HIGHEST, preferred_element_type=jnp.float32
        )
        grams[step, cam] = jnp.concatenate(
            [gram[f * tall : (f + 1) * tall] for f in range(folds)], axis=1
        )
        for peer in cam_peers:
            slot = grams.at[step, cam]
            send(slot, slot, gram_send.at[step, peer], gram_recv.at[step, cam], (peer, proj))
        for s in line[1:] + [spot]:
            to_pair(s)

        for s in line:
            for h in range(CUTS):
                line_out[step, s, h] = product(2 * s + side, h) + from_pair(s, h)
                send(
                    line_out.at[step, s, h],
                    line_in.at[step, spot, h],
                    line_send.at[step, s, h],
                    line_recv.at[step, spot, h],
                    (2 * s + side, proj),
                )
        for peer in cam_peers:
            arrived(grams.at[step, peer], gram_send.at[step, peer], gram_recv.at[step, peer])
        folded = grams[step, 0]
        for c in range(1, cams):
            folded += grams[step, c]
        folded = folded / (rows * cams)
        left = jnp.concatenate(
            [folded[:, f * rank : (f + 1) * rank] for f in range(folds)], axis=0
        )
        row = lax.broadcasted_iota(jnp.int32, (rank, rank), 0)
        col = lax.broadcasted_iota(jnp.int32, (rank, rank), 1)
        identity = jnp.where(row == col, 1.0, 0.0).astype(jnp.float32)
        left, right = eliminate(left, identity, 0, rank)
        inverse = inverse_factor(left, right)
        sums = [product(cam, h) + from_pair(spot, h) for h in range(CUTS)]
        basis_ref[...] = jnp.dot(
            inverse, sketch, precision=HIGHEST, preferred_element_type=jnp.float32
        )

        for h in range(CUTS):
            for s in line:
                arrived(line_in.at[step, s, h], line_send.at[step, s, h], line_recv.at[step, s, h])
                sums[h] += line_in[step, s, h]
        summed = jnp.concatenate(sums, axis=1)
        coimage = jnp.dot(inverse, summed, precision=HIGHEST, preferred_element_type=jnp.float32)
        coimage_ref[...] = coimage
        panels[step + 1, cam] = coimage.astype(jnp.bfloat16)
        for copy in sends:
            copy.wait_send()
        return carry

    lax.fori_loop(0, ITERS, one_pass, 0)


def deliver(basis_ref, coimage_ref, basis_out, coimage_out, sem):
    writes = [
        pltpu.make_async_copy(basis_ref, basis_out, sem.at[0]),
        pltpu.make_async_copy(coimage_ref, coimage_out, sem.at[1]),
    ]
    for write in writes:
        write.start()
    for write in writes:
        write.wait()


def with_kernel(cams, projs, transport, test_panel):
    rows, columns = transport.shape
    piece, rank = test_panel.shape
    dma = pltpu.SemaphoreType.DMA
    in_vmem = pl.BlockSpec(memory_space=pltpu.VMEM)
    anywhere = pl.BlockSpec(memory_space=pl.ANY)
    in_hbm = pl.BlockSpec(memory_space=pltpu.HBM)
    results = (pltpu.HBM((rank, rows), jnp.float32), pltpu.HBM((rank, piece), jnp.float32))
    kept = (pltpu.VMEM((rank, rows), jnp.float32), pltpu.VMEM((rank, piece), jnp.float32))
    exchanged = pltpu.VMEM((ITERS, cams // 2, CUTS, rank, piece // CUTS), jnp.float32)
    basis, coimage = pl.pallas_call(
        functools.partial(kernel, cams, projs),
        out_shape=kept,
        in_specs=[anywhere, in_vmem],
        out_specs=(in_vmem, in_vmem),
        scratch_shapes=[
            pltpu.VMEM((cams, rows, piece), jnp.bfloat16),
            pltpu.VMEM((ITERS + 1, cams, rank, piece), jnp.bfloat16),
            pltpu.VMEM((ITERS, 2, rank, rows), jnp.float32),
            pltpu.VMEM((ITERS, projs // 2, rank, rows), jnp.float32),
            pltpu.VMEM((ITERS, cams, rank * rank // 128, 128), jnp.float32),
            exchanged,
            exchanged,
            exchanged,
            exchanged,
            dma((cams,)),
            dma((ITERS, cams)),
            dma((ITERS, cams)),
            dma((ITERS, 1)),
            dma((ITERS, 1)),
            dma((ITERS, projs // 2)),
            dma((ITERS, projs // 2)),
            dma((ITERS, cams)),
            dma((ITERS, cams)),
            dma((ITERS, cams // 2, CUTS)),
            dma((ITERS, cams // 2, CUTS)),
            dma((ITERS, cams // 2, CUTS)),
            dma((ITERS, cams // 2, CUTS)),
        ],
        compiler_params=pltpu.CompilerParams(
            collective_id=0, has_side_effects=True, vmem_limit_bytes=60 * 2**20
        ),
        cost_estimate=pl.CostEstimate(
            flops=4 * ITERS * rows * columns * rank,
            bytes_accessed=2 * rows * columns,
            transcendentals=0,
        ),
    )(transport, test_panel.T)
    basis, coimage = pl.pallas_call(
        deliver,
        out_shape=results,
        in_specs=[in_vmem, in_vmem],
        out_specs=(in_hbm, in_hbm),
        scratch_shapes=[dma((2,))],
    )(basis, coimage)
    return basis.T, coimage.T


def solution(mesh):
    cams, projs = mesh.shape["cam"], mesh.shape["proj"]

    def on_device(transport, test_panel):
        if test_panel.shape[0] % (128 * CUTS) or transport.shape[0] % 128 or cams % 2 or projs % 2:
            return with_collectives(transport, test_panel)
        return with_kernel(cams, projs, transport, test_panel)

    return jax.shard_map(
        on_device,
        mesh=mesh,
        in_specs=(P("cam", "proj"), P(("proj", "cam"), None)),
        out_specs=(P("cam", None), P(("proj", "cam"), None)),
        check_vma=False,
    )
```

```python
import functools

import jax
import jax.numpy as jnp
from jax import lax
from jax.experimental import pallas as pl
from jax.experimental.pallas import tpu as pltpu
from jax.sharding import PartitionSpec as P

ITERS = 2
CUTS = 2
MESH = pl.DeviceIdType.MESH
HIGHEST = lax.Precision.HIGHEST
NT = (((1,), (1,)), ((), ()))


def small_gram(block):
    return jnp.dot(block.T, block, precision=HIGHEST, preferred_element_type=jnp.float32)


def apply_factor(gram, block):
    lower = jnp.linalg.cholesky(gram)
    return jax.scipy.linalg.solve_triangular(lower, block.T, lower=True).T


def with_collectives(transport, test_panel):
    total_rows = transport.shape[0] * lax.axis_size("cam")
    panel_piece = test_panel
    for step in range(ITERS):
        partial_sketch = jnp.dot(
            transport,
            lax.all_gather(panel_piece, "cam", axis=0, tiled=True),
            preferred_element_type=jnp.float32,
        )
        sketch = lax.psum(partial_sketch, "proj")
        gram = lax.psum(small_gram(sketch), "cam") / total_rows
        basis = apply_factor(gram, sketch)
        coimage = lax.psum_scatter(
            lax.dot_general(
                transport,
                basis.astype(jnp.bfloat16),
                (((0,), (0,)), ((), ())),
                preferred_element_type=jnp.float32,
            ),
            "cam",
            scatter_dimension=0,
            tiled=True,
        )
        panel_piece = coimage.astype(jnp.bfloat16)
    return basis, coimage


def eliminate(left, right, start, stop):
    row = lax.broadcasted_iota(jnp.int32, (left.shape[0], 1), 0)
    for k in range(start, stop):
        ratio = left[:, k : k + 1] / left[k : k + 1, k : k + 1]
        ratio = jnp.where(row > k, ratio, 0.0)
        right = right - ratio * right[k : k + 1, :]
        left = left - ratio * left[k : k + 1, :]
    return left, right


def inverse_factor(left, right):
    row = lax.broadcasted_iota(jnp.int32, left.shape, 0)
    col = lax.broadcasted_iota(jnp.int32, left.shape, 1)
    pivots = jnp.sum(jnp.where(row == col, left, 0.0), axis=1, keepdims=True)
    return right / jnp.sqrt(pivots)


def kernel(
    cams,
    projs,
    transport_ref,
    panel_ref,
    basis_ref,
    coimage_ref,
    transport,
    panels,
    partials,
    duos,
    grams,
    pair_out,
    pair_in,
    line_out,
    line_in,
    load_sem,
    panel_send,
    panel_recv,
    partial_send,
    partial_recv,
    duo_send,
    duo_recv,
    gram_send,
    gram_recv,
    pair_send,
    pair_recv,
    line_send,
    line_recv,
):
    cam, proj = lax.axis_index("cam"), lax.axis_index("proj")
    rank, piece = panel_ref.shape
    rows = transport.shape[1]
    width = piece // CUTS

    spots = cams // 2
    spot, side = cam // 2, lax.rem(cam, 2)
    other = 1 - side
    pair = 2 * spot + other
    offsets = sorted(range(1, spots), key=lambda o: -min(o, spots - o))
    line = [lax.rem(spot + o, spots) for o in offsets]
    cam_peers = [lax.rem(cam + o, cams) for o in range(1, cams)]
    duo, core = proj // 2, lax.rem(proj, 2)
    sibling = 2 * duo + 1 - core
    other_duos = [lax.rem(duo + o, projs // 2) for o in range(1, projs // 2)]
    proj_peers = [sibling] + [2 * d + core for d in other_duos]

    loads = []
    for c in range(cams):
        load = pltpu.make_async_copy(
            transport_ref.at[:, pl.ds(c * piece, piece)], transport.at[c], load_sem.at[c]
        )
        load.start()
        loads.append(load)

    barrier = pltpu.get_barrier_semaphore()
    for peer in cam_peers:
        pl.semaphore_signal(barrier, inc=1, device_id=(peer, proj), device_id_type=MESH)
    for peer in proj_peers:
        pl.semaphore_signal(barrier, inc=1, device_id=(cam, peer), device_id_type=MESH)
    panels[0, cam] = panel_ref[...]
    pl.semaphore_wait(barrier, cams - 1 + projs // 2)

    def copy_of(src, dst, send_sem, recv_sem, device):
        return pltpu.make_async_remote_copy(
            src_ref=src,
            dst_ref=dst,
            send_sem=send_sem,
            recv_sem=recv_sem,
            device_id=device,
            device_id_type=MESH,
        )

    def arrived(slot, send_sem, recv_sem):
        copy_of(slot, slot, send_sem, recv_sem, (pair, proj)).wait_recv()

    folds = 128 // rank
    tall = rank // folds

    def one_pass(step, carry):
        sends = []

        def send(*parts):
            copy = copy_of(*parts)
            copy.start()
            sends.append(copy)

        def share(c, peer, sem):
            slot = panels.at[step, c]
            send(slot, slot, panel_send.at[step, sem], panel_recv.at[step, c], (peer, proj))

        def wait_panel(c):
            arrived(panels.at[step, c], panel_send.at[step, c], panel_recv.at[step, c])

        def sketched(c):
            return lax.dot_general(
                panels[step, c], transport[c], NT, preferred_element_type=jnp.float32
            )

        for s in line:
            share(cam, 2 * s + side, 2 * s + side)
        share(cam, pair, pair)

        @pl.when(step == 0)
        def _():
            for load in loads:
                load.wait()

        total = sketched(cam)
        for s in reversed(line):
            wait_panel(2 * s + side)
            share(2 * s + side, pair, 2 * s + other)
            total += sketched(2 * s + side)
        wait_panel(pair)
        total += sketched(pair)
        for s in reversed(line):
            wait_panel(2 * s + other)
            total += sketched(2 * s + other)
        partials[step, core] = total
        slot = partials.at[step, core]
        send(slot, slot, partial_send.at[step, 0], partial_recv.at[step, 0], (cam, sibling))
        arrived(partials.at[step, 1 - core], partial_send.at[step, 0], partial_recv.at[step, 0])
        duos[step, duo] = partials[step, 0] + partials[step, 1]
        for d in other_duos:
            slot = duos.at[step, duo]
            send(slot, slot, duo_send.at[step, d], duo_recv.at[step, duo], (cam, 2 * d + core))
        for d in other_duos:
            arrived(duos.at[step, d], duo_send.at[step, d], duo_recv.at[step, d])
        sketch = duos[step, 0]
        for d in range(1, projs // 2):
            sketch += duos[step, d]

        high = sketch.astype(jnp.bfloat16)
        low = (sketch - high.astype(jnp.float32)).astype(jnp.bfloat16)
        both = jnp.concatenate([high, low], axis=0)

        def product(c, h):
            block = transport[c, :, h * width : (h + 1) * width]
            halves = jnp.dot(both, block, preferred_element_type=jnp.float32)
            return halves[:rank] + halves[rank:]

        def to_pair(s):
            for h in range(CUTS):
                pair_out[step, s, h] = product(2 * s + other, h)
                send(
                    pair_out.at[step, s, h],
                    pair_in.at[step, s, h],
                    pair_send.at[step, s, h],
                    pair_recv.at[step, s, h],
                    (pair, proj),
                )

        def from_pair(s, h):
            arrived(pair_in.at[step, s, h], pair_send.at[step, s, h], pair_recv.at[step, s, h])
            return pair_in[step, s, h]

        to_pair(line[0])
        gram = lax.dot_general(
            sketch, sketch, NT, precision=HIGHEST, preferred_element_type=jnp.float32
        )
        grams[step, cam] = jnp.concatenate(
            [gram[f * tall : (f + 1) * tall] for f in range(folds)], axis=1
        )
        for peer in cam_peers:
            slot = grams.at[step, cam]
            send(slot, slot, gram_send.at[step, peer], gram_recv.at[step, cam], (peer, proj))
        for s in line[1:] + [spot]:
            to_pair(s)

        for s in line:
            for h in range(CUTS):
                line_out[step, s, h] = product(2 * s + side, h) + from_pair(s, h)
                send(
                    line_out.at[step, s, h],
                    line_in.at[step, spot, h],
                    line_send.at[step, s, h],
                    line_recv.at[step, spot, h],
                    (2 * s + side, proj),
                )
        for peer in cam_peers:
            arrived(grams.at[step, peer], gram_send.at[step, peer], gram_recv.at[step, peer])
        folded = grams[step, 0]
        for c in range(1, cams):
            folded += grams[step, c]
        folded = folded / (rows * cams)
        left = jnp.concatenate(
            [folded[:, f * rank : (f + 1) * rank] for f in range(folds)], axis=0
        )
        row = lax.broadcasted_iota(jnp.int32, (rank, rank), 0)
        col = lax.broadcasted_iota(jnp.int32, (rank, rank), 1)
        identity = jnp.where(row == col, 1.0, 0.0).astype(jnp.float32)
        left, right = eliminate(left, identity, 0, rank)
        inverse = inverse_factor(left, right)
        sums = [product(cam, h) + from_pair(spot, h) for h in range(CUTS)]
        basis_ref[...] = jnp.dot(
            inverse, sketch, precision=HIGHEST, preferred_element_type=jnp.float32
        )

        for h in range(CUTS):
            for s in line:
                arrived(line_in.at[step, s, h], line_send.at[step, s, h], line_recv.at[step, s, h])
                sums[h] += line_in[step, s, h]
        summed = jnp.concatenate(sums, axis=1)
        coimage = jnp.dot(inverse, summed, precision=HIGHEST, preferred_element_type=jnp.float32)
        coimage_ref[...] = coimage
        panels[step + 1, cam] = coimage.astype(jnp.bfloat16)
        for copy in sends:
            copy.wait_send()
        return carry

    lax.fori_loop(0, ITERS, one_pass, 0)


def deliver(basis_ref, coimage_ref, basis_out, coimage_out, sem):
    writes = [
        pltpu.make_async_copy(basis_ref, basis_out, sem.at[0]),
        pltpu.make_async_copy(coimage_ref, coimage_out, sem.at[1]),
    ]
    for write in writes:
        write.start()
    for write in writes:
        write.wait()


def with_kernel(cams, projs, transport, test_panel):
    rows, columns = transport.shape
    piece, rank = test_panel.shape
    dma = pltpu.SemaphoreType.DMA
    in_vmem = pl.BlockSpec(memory_space=pltpu.VMEM)
    anywhere = pl.BlockSpec(memory_space=pl.ANY)
    in_hbm = pl.BlockSpec(memory_space=pltpu.HBM)
    results = (pltpu.HBM((rank, rows), jnp.float32), pltpu.HBM((rank, piece), jnp.float32))
    kept = (pltpu.VMEM((rank, rows), jnp.float32), pltpu.VMEM((rank, piece), jnp.float32))
    exchanged = pltpu.VMEM((ITERS, cams // 2, CUTS, rank, piece // CUTS), jnp.float32)
    basis, coimage = pl.pallas_call(
        functools.partial(kernel, cams, projs),
        out_shape=kept,
        in_specs=[anywhere, in_vmem],
        out_specs=(in_vmem, in_vmem),
        scratch_shapes=[
            pltpu.VMEM((cams, rows, piece), jnp.bfloat16),
            pltpu.VMEM((ITERS + 1, cams, rank, piece), jnp.bfloat16),
            pltpu.VMEM((ITERS, 2, rank, rows), jnp.float32),
            pltpu.VMEM((ITERS, projs // 2, rank, rows), jnp.float32),
            pltpu.VMEM((ITERS, cams, rank * rank // 128, 128), jnp.float32),
            exchanged,
            exchanged,
            exchanged,
            exchanged,
            dma((cams,)),
            dma((ITERS, cams)),
            dma((ITERS, cams)),
            dma((ITERS, 1)),
            dma((ITERS, 1)),
            dma((ITERS, projs // 2)),
            dma((ITERS, projs // 2)),
            dma((ITERS, cams)),
            dma((ITERS, cams)),
            dma((ITERS, cams // 2, CUTS)),
            dma((ITERS, cams // 2, CUTS)),
            dma((ITERS, cams // 2, CUTS)),
            dma((ITERS, cams // 2, CUTS)),
        ],
        compiler_params=pltpu.CompilerParams(
            collective_id=0, has_side_effects=True, vmem_limit_bytes=60 * 2**20
        ),
        cost_estimate=pl.CostEstimate(
            flops=4 * ITERS * rows * columns * rank,
            bytes_accessed=2 * rows * columns,
            transcendentals=0,
        ),
    )(transport, test_panel.T)
    basis, coimage = pl.pallas_call(
        deliver,
        out_shape=results,
        in_specs=[in_vmem, in_vmem],
        out_specs=(in_hbm, in_hbm),
        scratch_shapes=[dma((2,))],
        compiler_params=pltpu.CompilerParams(vmem_limit_bytes=2**20),
    )(basis, coimage)
    return basis.T, coimage.T


def solution(mesh):
    cams, projs = mesh.shape["cam"], mesh.shape["proj"]

    def on_device(transport, test_panel):
        if test_panel.shape[0] % (128 * CUTS) or transport.shape[0] % 128 or cams % 2 or projs % 2:
            return with_collectives(transport, test_panel)
        return with_kernel(cams, projs, transport, test_panel)

    return jax.shard_map(
        on_device,
        mesh=mesh,
        in_specs=(P("cam", "proj"), P(("proj", "cam"), None)),
        out_specs=(P("cam", None), P(("proj", "cam"), None)),
        check_vma=False,
    )
```

```python
import functools

import jax
import jax.numpy as jnp
from jax import lax
from jax.experimental import pallas as pl
from jax.experimental.pallas import tpu as pltpu
from jax.sharding import PartitionSpec as P

ITERS = 2
CUTS = 2
MESH = pl.DeviceIdType.MESH
HIGHEST = lax.Precision.HIGHEST
NT = (((1,), (1,)), ((), ()))


def small_gram(block):
    return jnp.dot(block.T, block, precision=HIGHEST, preferred_element_type=jnp.float32)


def apply_factor(gram, block):
    lower = jnp.linalg.cholesky(gram)
    return jax.scipy.linalg.solve_triangular(lower, block.T, lower=True).T


def with_collectives(transport, test_panel):
    total_rows = transport.shape[0] * lax.axis_size("cam")
    panel_piece = test_panel
    for step in range(ITERS):
        partial_sketch = jnp.dot(
            transport,
            lax.all_gather(panel_piece, "cam", axis=0, tiled=True),
            preferred_element_type=jnp.float32,
        )
        sketch = lax.psum(partial_sketch, "proj")
        gram = lax.psum(small_gram(sketch), "cam") / total_rows
        basis = apply_factor(gram, sketch)
        coimage = lax.psum_scatter(
            lax.dot_general(
                transport,
                basis.astype(jnp.bfloat16),
                (((0,), (0,)), ((), ())),
                preferred_element_type=jnp.float32,
            ),
            "cam",
            scatter_dimension=0,
            tiled=True,
        )
        panel_piece = coimage.astype(jnp.bfloat16)
    return basis, coimage


def eliminate(left, right, start, stop):
    row = lax.broadcasted_iota(jnp.int32, (left.shape[0], 1), 0)
    for k in range(start, stop):
        ratio = left[:, k : k + 1] / left[k : k + 1, k : k + 1]
        ratio = jnp.where(row > k, ratio, 0.0)
        right = right - ratio * right[k : k + 1, :]
        left = left - ratio * left[k : k + 1, :]
    return left, right


def inverse_factor(left, right):
    row = lax.broadcasted_iota(jnp.int32, left.shape, 0)
    col = lax.broadcasted_iota(jnp.int32, left.shape, 1)
    pivots = jnp.sum(jnp.where(row == col, left, 0.0), axis=1, keepdims=True)
    return right / jnp.sqrt(pivots)


def kernel(
    cams,
    projs,
    transport_ref,
    panel_ref,
    basis_ref,
    coimage_ref,
    transport,
    panels,
    partials,
    duos,
    grams,
    pair_out,
    pair_in,
    line_out,
    line_in,
    load_sem,
    panel_send,
    panel_recv,
    partial_send,
    partial_recv,
    duo_send,
    duo_recv,
    gram_send,
    gram_recv,
    pair_send,
    pair_recv,
    line_send,
    line_recv,
):
    cam, proj = lax.axis_index("cam"), lax.axis_index("proj")
    rank, piece = panel_ref.shape
    rows = transport.shape[1]
    width = piece // CUTS

    spots = cams // 2
    spot, side = cam // 2, lax.rem(cam, 2)
    other = 1 - side
    pair = 2 * spot + other
    offsets = sorted(range(1, spots), key=lambda o: -min(o, spots - o))
    line = [lax.rem(spot + o, spots) for o in offsets]
    arrivals = line[:1] + line[:0:-1]
    cam_peers = [lax.rem(cam + o, cams) for o in range(1, cams)]
    duo, core = proj // 2, lax.rem(proj, 2)
    sibling = 2 * duo + 1 - core
    other_duos = [lax.rem(duo + o, projs // 2) for o in range(1, projs // 2)]
    proj_peers = [sibling] + [2 * d + core for d in other_duos]

    loads = []
    for c in range(cams):
        load = pltpu.make_async_copy(
            transport_ref.at[:, pl.ds(c * piece, piece)], transport.at[c], load_sem.at[c]
        )
        load.start()
        loads.append(load)

    barrier = pltpu.get_barrier_semaphore()
    for peer in cam_peers:
        pl.semaphore_signal(barrier, inc=1, device_id=(peer, proj), device_id_type=MESH)
    for peer in proj_peers:
        pl.semaphore_signal(barrier, inc=1, device_id=(cam, peer), device_id_type=MESH)
    panels[0, cam] = panel_ref[...]
    pl.semaphore_wait(barrier, cams - 1 + projs // 2)

    def copy_of(src, dst, send_sem, recv_sem, device):
        return pltpu.make_async_remote_copy(
            src_ref=src,
            dst_ref=dst,
            send_sem=send_sem,
            recv_sem=recv_sem,
            device_id=device,
            device_id_type=MESH,
        )

    def arrived(slot, send_sem, recv_sem):
        copy_of(slot, slot, send_sem, recv_sem, (pair, proj)).wait_recv()

    folds = 128 // rank
    tall = rank // folds

    def one_pass(step, carry):
        sends = []

        def send(*parts):
            copy = copy_of(*parts)
            copy.start()
            sends.append(copy)

        def share(c, peer, sem):
            slot = panels.at[step, c]
            send(slot, slot, panel_send.at[step, sem], panel_recv.at[step, c], (peer, proj))

        def wait_panel(c):
            arrived(panels.at[step, c], panel_send.at[step, c], panel_recv.at[step, c])

        def sketched(c):
            return lax.dot_general(
                panels[step, c], transport[c], NT, preferred_element_type=jnp.float32
            )

        for s in line:
            share(cam, 2 * s + side, 2 * s + side)
        share(cam, pair, pair)

        @pl.when(step == 0)
        def _():
            for load in loads:
                load.wait()

        total = sketched(cam)
        for s in arrivals:
            wait_panel(2 * s + side)
            share(2 * s + side, pair, 2 * s + other)
            total += sketched(2 * s + side)
        wait_panel(pair)
        total += sketched(pair)
        for s in arrivals:
            wait_panel(2 * s + other)
            total += sketched(2 * s + other)
        partials[step, core] = total
        slot = partials.at[step, core]
        send(slot, slot, partial_send.at[step, 0], partial_recv.at[step, 0], (cam, sibling))
        arrived(partials.at[step, 1 - core], partial_send.at[step, 0], partial_recv.at[step, 0])
        duos[step, duo] = partials[step, 0] + partials[step, 1]
        for d in other_duos:
            slot = duos.at[step, duo]
            send(slot, slot, duo_send.at[step, d], duo_recv.at[step, duo], (cam, 2 * d + core))
        for d in other_duos:
            arrived(duos.at[step, d], duo_send.at[step, d], duo_recv.at[step, d])
        sketch = duos[step, 0]
        for d in range(1, projs // 2):
            sketch += duos[step, d]

        high = sketch.astype(jnp.bfloat16)
        low = (sketch - high.astype(jnp.float32)).astype(jnp.bfloat16)
        both = jnp.concatenate([high, low], axis=0)

        def product(c, h):
            block = transport[c, :, h * width : (h + 1) * width]
            halves = jnp.dot(both, block, preferred_element_type=jnp.float32)
            return halves[:rank] + halves[rank:]

        def to_pair(s):
            for h in range(CUTS):
                pair_out[step, s, h] = product(2 * s + other, h)
                send(
                    pair_out.at[step, s, h],
                    pair_in.at[step, s, h],
                    pair_send.at[step, s, h],
                    pair_recv.at[step, s, h],
                    (pair, proj),
                )

        def from_pair(s, h):
            arrived(pair_in.at[step, s, h], pair_send.at[step, s, h], pair_recv.at[step, s, h])
            return pair_in[step, s, h]

        to_pair(line[0])
        gram = lax.dot_general(
            sketch, sketch, NT, precision=HIGHEST, preferred_element_type=jnp.float32
        )
        grams[step, cam] = jnp.concatenate(
            [gram[f * tall : (f + 1) * tall] for f in range(folds)], axis=1
        )
        for peer in cam_peers:
            slot = grams.at[step, cam]
            send(slot, slot, gram_send.at[step, peer], gram_recv.at[step, cam], (peer, proj))
        for s in line[1:] + [spot]:
            to_pair(s)

        for s in line:
            for h in range(CUTS):
                line_out[step, s, h] = product(2 * s + side, h) + from_pair(s, h)
                send(
                    line_out.at[step, s, h],
                    line_in.at[step, spot, h],
                    line_send.at[step, s, h],
                    line_recv.at[step, spot, h],
                    (2 * s + side, proj),
                )
        for peer in cam_peers:
            arrived(grams.at[step, peer], gram_send.at[step, peer], gram_recv.at[step, peer])
        folded = grams[step, 0]
        for c in range(1, cams):
            folded += grams[step, c]
        folded = folded / (rows * cams)
        left = jnp.concatenate(
            [folded[:, f * rank : (f + 1) * rank] for f in range(folds)], axis=0
        )
        row = lax.broadcasted_iota(jnp.int32, (rank, rank), 0)
        col = lax.broadcasted_iota(jnp.int32, (rank, rank), 1)
        identity = jnp.where(row == col, 1.0, 0.0).astype(jnp.float32)
        left, right = eliminate(left, identity, 0, rank)
        inverse = inverse_factor(left, right)
        sums = [product(cam, h) + from_pair(spot, h) for h in range(CUTS)]
        basis_ref[...] = jnp.dot(
            inverse, sketch, precision=HIGHEST, preferred_element_type=jnp.float32
        )

        for h in range(CUTS):
            for s in line:
                arrived(line_in.at[step, s, h], line_send.at[step, s, h], line_recv.at[step, s, h])
                sums[h] += line_in[step, s, h]
        summed = jnp.concatenate(sums, axis=1)
        coimage = jnp.dot(inverse, summed, precision=HIGHEST, preferred_element_type=jnp.float32)
        coimage_ref[...] = coimage
        panels[step + 1, cam] = coimage.astype(jnp.bfloat16)
        for copy in sends:
            copy.wait_send()
        return carry

    lax.fori_loop(0, ITERS, one_pass, 0)


def deliver(basis_ref, coimage_ref, basis_out, coimage_out, sem):
    writes = [
        pltpu.make_async_copy(basis_ref, basis_out, sem.at[0]),
        pltpu.make_async_copy(coimage_ref, coimage_out, sem.at[1]),
    ]
    for write in writes:
        write.start()
    for write in writes:
        write.wait()


def with_kernel(cams, projs, transport, test_panel):
    rows, columns = transport.shape
    piece, rank = test_panel.shape
    dma = pltpu.SemaphoreType.DMA
    in_vmem = pl.BlockSpec(memory_space=pltpu.VMEM)
    anywhere = pl.BlockSpec(memory_space=pl.ANY)
    in_hbm = pl.BlockSpec(memory_space=pltpu.HBM)
    results = (pltpu.HBM((rank, rows), jnp.float32), pltpu.HBM((rank, piece), jnp.float32))
    kept = (pltpu.VMEM((rank, rows), jnp.float32), pltpu.VMEM((rank, piece), jnp.float32))
    exchanged = pltpu.VMEM((ITERS, cams // 2, CUTS, rank, piece // CUTS), jnp.float32)
    basis, coimage = pl.pallas_call(
        functools.partial(kernel, cams, projs),
        out_shape=kept,
        in_specs=[anywhere, in_vmem],
        out_specs=(in_vmem, in_vmem),
        scratch_shapes=[
            pltpu.VMEM((cams, rows, piece), jnp.bfloat16),
            pltpu.VMEM((ITERS + 1, cams, rank, piece), jnp.bfloat16),
            pltpu.VMEM((ITERS, 2, rank, rows), jnp.float32),
            pltpu.VMEM((ITERS, projs // 2, rank, rows), jnp.float32),
            pltpu.VMEM((ITERS, cams, rank * rank // 128, 128), jnp.float32),
            exchanged,
            exchanged,
            exchanged,
            exchanged,
            dma((cams,)),
            dma((ITERS, cams)),
            dma((ITERS, cams)),
            dma((ITERS, 1)),
            dma((ITERS, 1)),
            dma((ITERS, projs // 2)),
            dma((ITERS, projs // 2)),
            dma((ITERS, cams)),
            dma((ITERS, cams)),
            dma((ITERS, cams // 2, CUTS)),
            dma((ITERS, cams // 2, CUTS)),
            dma((ITERS, cams // 2, CUTS)),
            dma((ITERS, cams // 2, CUTS)),
        ],
        compiler_params=pltpu.CompilerParams(
            collective_id=0, has_side_effects=True, vmem_limit_bytes=60 * 2**20
        ),
        cost_estimate=pl.CostEstimate(
            flops=4 * ITERS * rows * columns * rank,
            bytes_accessed=2 * rows * columns,
            transcendentals=0,
        ),
    )(transport, test_panel.T)
    basis, coimage = pl.pallas_call(
        deliver,
        out_shape=results,
        in_specs=[in_vmem, in_vmem],
        out_specs=(in_hbm, in_hbm),
        scratch_shapes=[dma((2,))],
        compiler_params=pltpu.CompilerParams(vmem_limit_bytes=2**20),
    )(basis, coimage)
    return basis.T, coimage.T


def solution(mesh):
    cams, projs = mesh.shape["cam"], mesh.shape["proj"]

    def on_device(transport, test_panel):
        if test_panel.shape[0] % (128 * CUTS) or transport.shape[0] % 128 or cams % 2 or projs % 2:
            return with_collectives(transport, test_panel)
        return with_kernel(cams, projs, transport, test_panel)

    return jax.shard_map(
        on_device,
        mesh=mesh,
        in_specs=(P("cam", "proj"), P(("proj", "cam"), None)),
        out_specs=(P("cam", None), P(("proj", "cam"), None)),
        check_vma=False,
    )
```
